128 devices in a mesh: segment: 2 (over core), cp: 16 (over x, z), tp: 4 (over y).
Axes of the slice: x: 4, y: 4, z: 4, core: 2. Of those that a mesh axis runs over, the one named last changes fastest.
Arguments:
- image_rows: bfloat16 [32, 801, 8192], P('cp', None, ('segment', 'tp')), may hold values from -6 to 6
- kv_weight: bfloat16 [8192, 2048], P(('segment', 'tp')), may hold values from -0.0625 to 0.0625
- k_gain: float32 [128], replicated, may hold values from 1 to 2.2
- tokens: bfloat16 [2048, 8192], P('cp', ('segment', 'tp')), may hold values from -6 to 6
- ln_gain: float32 [8192], replicated, may hold values from 0.1 to 1.9
- q_weight: bfloat16 [8192, 8192], P(None, ('segment', 'tp')), may hold values from -0.0625 to 0.0625
- q_gain: float32 [128], replicated, may hold values from 1 to 2.2
- image_doc: int32 [32], replicated, may hold values from 0 to 31, as said below
- doc_first: int32 [32], replicated, may hold values from 0 to 15, as said below
- doc_count: int32 [32], replicated, may hold values from 1 to 8, as said below
- token_mask: int32 [2048, 32], P('cp'), may hold values 0 or 1
Outputs:
- attended: bfloat16 [2048, 8192], P('cp', ('segment', 'tp'))
The draws below stay inside these ranges and needn't reach their ends.
Inputs may be any that keep to these rules, and one draw needn't show every extreme that they name: `image_doc`: A permutation: each document holds exactly one image. `doc_first`: the documents of the 2 images of one context shard h (images h * 2 to h * 2 + 1) cover pairwise disjoint sets of context shards, so no context shard is covered by two images of the same shard. Some document starts on the last context shard. doc_first + doc_count never exceeds the number of context shards; some document covers exactly 16 // 2 shards and some exactly one.
All inputs are finite; a program needn't handle non-finite values. No bound on the sum of `token_mask` on one device may be relied on, other than what follows from the above.
Results may differ from the reference program's by a relative error of at most 0.034.
Values may be sent and summed in bfloat16 or wider, within the bound.
A program may use at most 128 MiB of HBM per device.

```python
import math
import jax
import jax.numpy as jnp
from jax import lax

D = 8192
HEADS = 64
KV_HEADS = 8
HD = 128
VW = 8192
IMG_TOK = 801
IMG_DEV = 2
TOK_DEV = 128
TOKENS = 2048
IMAGES = 32
DOCS = 32
N_SEGMENT = 2
N_CP = 16
N_TP = 4


def routing(key):
    shards = IMAGES // IMG_DEV
    reach_most = shards // IMG_DEV
    span_least = max(1, reach_most // 2)
    key_shuffle = jax.random.fold_in(key, 11)
    key_offsets = jax.random.fold_in(key, 12)
    key_spans = jax.random.fold_in(key, 13)
    key_turns = jax.random.fold_in(key, 14)
    shuffle = jax.random.permutation(key_shuffle, IMAGES).astype(jnp.int32)
    image_ids = jnp.arange(IMAGES, dtype=jnp.int32)
    source = image_ids // IMG_DEV
    slot_index = image_ids % IMG_DEV
    turns = jax.random.randint(key_turns, (shards,), 0, IMG_DEV, dtype=jnp.int32)
    window = (slot_index + turns[source]) % IMG_DEV
    spans = jax.random.randint(key_spans, (IMAGES,), span_least, reach_most + 1, dtype=jnp.int32)
    spans = spans.at[0].set(reach_most)
    last_pick = (source == 1) & (window == IMG_DEV - 1)
    spans = jnp.where(last_pick, 1, spans).astype(jnp.int32)
    raw_offsets = jax.random.randint(key_offsets, (IMAGES,), 0, 1 << 20, dtype=jnp.int32)
    within = raw_offsets % (reach_most - spans + 1)
    within = jnp.where(last_pick, reach_most - 1, within).astype(jnp.int32)
    starts = window * reach_most + within
    inverse = jnp.argsort(shuffle).astype(jnp.int32)
    return (shuffle, starts[inverse], spans[inverse])


def draw_image_doc(key, part):
    shared = routing(key)
    return shared[0]


def draw_doc_first(key, part):
    shared = routing(key)
    return shared[1]


def draw_doc_count(key, part):
    shared = routing(key)
    return shared[2]


def touch_ends(array, rng, least, high):
    longest = array.shape.index(max(array.shape))
    spots = []
    for shift in (0, 1):
        where = [jax.random.randint(jax.random.fold_in(rng, axis), (), 0, length) for axis, length in enumerate(array.shape)]
        where[longest] = (where[longest] + shift) % array.shape[longest]
        spots.append(tuple(where))
    return array.at[spots[0]].set(least).at[spots[1]].set(high)


def shard_levels(rng, shape, split, low, largest):
    def one(position, shards_of):
        steps = jax.random.uniform(jax.random.fold_in(jax.random.fold_in(rng, 6), position), (shards_of,), jnp.float32, low / len(split), largest / len(split))
        return jnp.repeat(jnp.exp(steps), shape[position] // shards_of).reshape((-1,) + (1,) * (len(shape) - position - 1))

    loudness = one(*split[0])
    for cut in split[1:]:
        loudness = loudness * one(*cut)
    return loudness


def scatter_about(rng, dims, spread, limit, pieces=(), kind=jnp.bfloat16):
    drawn = spread * jax.random.normal(rng, dims, jnp.float32)
    if pieces:
        drawn = drawn * shard_levels(rng, dims, pieces, -0.22, 0.18)
    return jnp.clip(drawn, -limit, limit).astype(kind)


def setup_inputs(seed: int = 0) -> dict:
    key_list = jax.random.split(jax.random.key(seed), 12)
    return {
        "image_rows": scatter_about(key_list[0], (IMAGES, IMG_TOK, VW), 1.0, 6.0, ((0, 16), (2, 8))),
        "kv_weight": scatter_about(key_list[1], (VW, KV_HEADS * 2 * HD), VW ** -0.5, 0.0625, ((0, 8),)),
        "k_gain": jnp.clip(jnp.exp(jax.random.uniform(key_list[2], (HD,), jnp.float32, math.log(1.0), math.log(2.2))), 1.0, 2.2),
        "tokens": scatter_about(key_list[3], (TOKENS, D), 1.0, 6.0, ((0, 16), (1, 8))),
        "ln_gain": jnp.clip(1.0 + 0.18 * jax.random.normal(key_list[4], (D,), jnp.float32), 0.1, 1.9),
        "q_weight": scatter_about(key_list[5], (D, HEADS * HD), D ** -0.5, 0.0625, ((1, 8),)),
        "q_gain": jnp.clip(jnp.exp(jax.random.uniform(key_list[6], (HD,), jnp.float32, math.log(1.0), math.log(2.2))), 1.0, 2.2),
        "image_doc": draw_image_doc(jax.random.fold_in(key_list[11], 71), 0),
        "doc_first": draw_doc_first(jax.random.fold_in(key_list[11], 71), 0),
        "doc_count": draw_doc_count(jax.random.fold_in(key_list[11], 71), 0),
        "token_mask": touch_ends((jax.random.randint(key_list[10], (TOKENS, IMAGES), 0, 2) < 1).astype(jnp.int32), jax.random.fold_in(key_list[10], 1), 0, 1),
    }


EPSILON = 1e-06

def normalize(values_in):
    return values_in * lax.rsqrt(lax.optimization_barrier(jnp.mean(values_in * values_in, axis=-1, keepdims=True)) + EPSILON)

def reference(image_rows, kv_weight, k_gain, tokens, ln_gain, q_weight, q_gain, image_doc, doc_first, doc_count, token_mask):
    group_size = HEADS // KV_HEADS
    n_blocks = N_SEGMENT * N_TP
    block_width = VW // n_blocks
    kv_blocks = kv_weight.reshape(n_blocks, block_width, KV_HEADS * 2 * HD).astype(jnp.float32)

    def project(image):
        parts = image.reshape(IMG_TOK, n_blocks, block_width).astype(jnp.float32)
        partial_sums = jnp.einsum('tbv,bvc->btc', parts, kv_blocks)
        rounded_parts = lax.optimization_barrier(partial_sums.astype(jnp.bfloat16)).astype(jnp.float32)
        return lax.optimization_barrier(jnp.sum(rounded_parts, axis=0))
    projected = lax.map(project, image_rows)
    split_kv = projected.reshape(IMAGES, IMG_TOK, KV_HEADS, 2, HD)
    key_part = (normalize(split_kv[:, :, :, 0]) * k_gain).astype(jnp.bfloat16)
    value_part = split_kv[:, :, :, 1].astype(jnp.bfloat16)
    slabs = jnp.stack([key_part, value_part], axis=3).reshape(IMAGES, IMG_TOK, KV_HEADS * 2 * HD)
    scaled = (tokens * ln_gain).astype(jnp.bfloat16)
    query_raw = jnp.dot(scaled, q_weight, preferred_element_type=jnp.float32)
    query_raw = query_raw.reshape(TOKENS, KV_HEADS, group_size, HD)
    queries = (normalize(query_raw) * q_gain / math.sqrt(HD)).astype(jnp.bfloat16)
    matches = image_doc[:, None] == jnp.arange(DOCS, dtype=jnp.int32)[None, :]
    doc_start = lax.optimization_barrier(jnp.sum(jnp.where(matches, doc_first[None, :], 0), axis=1))
    doc_span = lax.optimization_barrier(jnp.sum(jnp.where(matches, doc_count[None, :], 0), axis=1))
    shard_ids = jnp.arange(N_CP, dtype=jnp.int32)
    cover = ((doc_start[:, None] <= shard_ids[None, :]) & (shard_ids[None, :] < (doc_start + doc_span)[:, None])).astype(jnp.float32)

    def one_shard(shard_idx):
        shard_q = lax.dynamic_slice_in_dim(queries, shard_idx * TOK_DEV, TOK_DEV, 0).astype(jnp.float32)
        tok_mask = lax.dynamic_slice_in_dim(token_mask, shard_idx * TOK_DEV, TOK_DEV, 0).astype(jnp.float32)
        cover_now = lax.dynamic_index_in_dim(cover, shard_idx, 1, keepdims=False)
        tok_weight = tok_mask * cover_now[None, :]

        def advance(carry_state, source):
            cover_part = lax.dynamic_slice_in_dim(cover_now, source * IMG_DEV, IMG_DEV, 0)

            def compute(current):
                numer, denom = current
                kv_block = lax.dynamic_slice_in_dim(slabs, source * IMG_DEV, IMG_DEV, 0).astype(jnp.float32)
                kv_slab = lax.optimization_barrier(jnp.sum(cover_part[:, None, None] * kv_block, axis=0)).reshape(IMG_TOK, KV_HEADS, 2, HD)
                slot_weight = lax.optimization_barrier(jnp.sum(lax.dynamic_slice_in_dim(tok_weight, source * IMG_DEV, IMG_DEV, 1), axis=1))
                scores = jnp.einsum('thgd,khd->thgk', shard_q, kv_slab[:, :, 0])
                weights_p = jnp.exp(scores) * slot_weight[:, None, None, None]
                rounded = lax.optimization_barrier(weights_p.astype(jnp.bfloat16)).astype(jnp.float32)
                numer = numer + jnp.einsum('thgk,khd->thgd', rounded, kv_slab[:, :, 1])
                denom = denom + lax.optimization_barrier(jnp.sum(weights_p, axis=-1))
                return (numer, denom)
            used_now = jnp.sum(cover_part) > 0
            return (lax.cond(used_now, compute, lambda current: current, carry_state), None)
        start_state = (jnp.zeros((TOK_DEV, KV_HEADS, group_size, HD), jnp.float32), jnp.zeros((TOK_DEV, KV_HEADS, group_size), jnp.float32))
        (numer, denom), _ = lax.scan(advance, start_state, jnp.arange(N_CP, dtype=jnp.int32))
        divisor = jnp.where(denom > 0, denom, 1.0)
        result = jnp.where(denom[..., None] > 0, numer / divisor[..., None], 0.0)
        return result.reshape(TOK_DEV, HEADS * HD).astype(jnp.bfloat16)
    return lax.map(one_shard, jnp.arange(N_CP, dtype=jnp.int32)).reshape(TOKENS, HEADS * HD)
```

```python
import functools
import math

import jax
import jax.numpy as jnp
from jax import lax
from jax.experimental import pallas as pl
from jax.experimental.pallas import tpu as pltpu
from jax.sharding import PartitionSpec as P

EPSILON = 1e-06
MESH = pl.DeviceIdType.MESH
BF16 = jnp.bfloat16
F32 = jnp.float32

RING = 4
SHARDS = 16
TOK = 128
HD = 128
IMG_TOK = 801
KV_ROWS = 816
KEYS = 896
HALF = 528
CUT = 256

KV_ORDER = ((2, 0), (2, 1), (1, 1), (3, 0), (1, 0), (3, 1), (0, 0), (0, 1))
UNITS = (
    (2, 2), (2, 1), (1, 2), (2, 3), (3, 2), (2, 0), (0, 2), (1, 1),
    (3, 3), (1, 3), (3, 1), (1, 0), (0, 1), (3, 0), (0, 3), (0, 0),
)
FAR_LAG = 3
NEAR_LAG = 5


def pick(index, values):
    return sum((index == at).astype(jnp.int32) * value for at, value in enumerate(values) if value)


def lay_out(unit_of):
    steps = []
    order = 0

    def add(slot, kind, half, dg):
        nonlocal order
        steps.append((slot, order, kind, half, dg))
        order += 1

    for half in (0, 1):
        unit = lambda df, dg: unit_of[(dg, df) if half == 0 else (df, dg)]
        total_at = {}
        for dg in (2, 1, 3, 0):
            far = unit(2, dg)
            add(far, "far", half, dg)
            up = max(unit(1, dg), far + FAR_LAG)
            down = max(unit(3, dg), far + FAR_LAG)
            add(up, "up", half, dg)
            add(down, "down", half, dg)
            total_at[dg] = max(unit(0, dg), max(up, down) + NEAR_LAG)
            add(total_at[dg], "total", half, dg)
        add(total_at[2], "gfar", half, 2)
        add(max(total_at[1], total_at[2] + FAR_LAG), "gup", half, 1)
        add(max(total_at[3], total_at[2] + FAR_LAG), "gdown", half, 3)
    return sorted(steps)


def kernel(
    x_hbm, w_hbm, kg_ref, tok_ref, ln_ref, wq_hbm, qg_ref, doc_ref, first_ref, count_ref, mask_ref,
    out_ref,
    xs, ws, wq, tok, cs, cr, mine, yr, acc, qall, kb, vb, pb, rf, rn, rgf, rgn, total,
    load_sem, send_sem, recv_sem,
):
    s = lax.axis_index("segment")
    cp = lax.axis_index("cp")
    t = lax.axis_index("tp")
    x, z = cp // RING, cp % RING

    def plus(v, n):
        return lax.rem(v + n, RING)

    peers = {
        "c": (1 - s, cp, t),
        "y+": (s, cp, plus(t, 1)),
        "y-": (s, cp, plus(t, 3)),
        "x+": (s, plus(x, 1) * RING + z, t),
        "x-": (s, plus(x, 3) * RING + z, t),
        "z+": (s, x * RING + plus(z, 1), t),
        "z-": (s, x * RING + plus(z, 3), t),
    }

    numbers = {}

    def number(key):
        return numbers.setdefault(key, len(numbers))

    started = []

    def copy_of(key, src, dst, peer):
        n = number(key) if isinstance(key, tuple) else key
        return pltpu.make_async_remote_copy(
            src_ref=src, dst_ref=dst, send_sem=send_sem.at[n], recv_sem=recv_sem.at[n],
            device_id=peers[peer], device_id_type=MESH,
        )

    def send(key, src, dst, peer):
        copy_of(key, src(), dst(), peer).start()
        started.append((key, src, dst, peer))

    def arrived(key, dst):
        copy_of(key, dst, dst, "c").wait_recv()

    def load(n, src, dst):
        return pltpu.make_async_copy(src, dst, load_sem.at[n])

    def head_cols(head):
        return pl.ds(pl.multiple_of(head * 2 * HD, 2 * HD), 2 * HD)

    x_loads = [load(i, x_hbm.at[i], xs.at[i]) for i in range(2)]
    w_loads = {}
    for at, dt in enumerate((2, 1, 3, 0)):
        for other in (1, 0):
            head = (1 - s if other else s) * RING + plus(t, dt)
            w_loads[dt, other] = load(
                2 + at * 2 + (1 - other), w_hbm.at[:, head_cols(head)], ws.at[at * 2 + (1 - other)]
            )
    tok_order = ((0, 0), (1, 0), (0, 3), (0, 1), (1, 3), (1, 1), (0, 2), (1, 2))
    blocks = [(1 - s if o else s) * RING + plus(t, dt) for o, dt in tok_order]
    width = wq.shape[0] // 8
    wq_loads = [
        load(10 + n, wq_hbm.at[pl.ds(pl.multiple_of(b * width, width), width)], wq.at[pl.ds(n * width, width)])
        for n, b in enumerate(blocks)
    ]
    x_loads[0].start()
    w_loads[2, 1].start()
    w_loads[2, 0].start()
    x_loads[1].start()
    for dt in (1, 3, 0):
        w_loads[dt, 1].start()
        w_loads[dt, 0].start()
    for copy in wq_loads:
        copy.start()

    barrier = pltpu.get_barrier_semaphore()
    for peer in peers.values():
        pl.semaphore_signal(barrier, inc=1, device_id=peer, device_id_type=MESH)

    gain = ln_ref[s * RING + t]
    for c in range(8):
        cols = slice(c * 128, (c + 1) * 128)
        tok[0, :, cols] = (tok_ref[:, cols].astype(F32) * gain[c : c + 1, :]).astype(BF16)
    pl.semaphore_wait(barrier, len(peers))

    send(("tok", "y+"), lambda: tok.at[0], lambda: tok.at[2], "y+")
    send(("tok", "y-"), lambda: tok.at[0], lambda: tok.at[3], "y-")
    send(("tok", "c0"), lambda: tok.at[0], lambda: tok.at[1], "c")

    cut = 400
    kv_c = [number(("kvc", k)) for k in range(8)]
    assert kv_c == list(range(kv_c[0], kv_c[0] + 8))

    def kv_slot(k, carry):
        dt_at = pick(k, [(2, 1, 3, 0).index(dt) for dt, _ in KV_ORDER])
        img = pick(k, [i for _, i in KV_ORDER])

        @pl.when(k == 0)
        def _():
            x_loads[0].wait()
            w_loads[2, 1].wait()
            w_loads[2, 0].wait()

        @pl.when(k == 1)
        def _():
            x_loads[1].wait()

        for first_use, dt in ((2, 1), (3, 3), (6, 0)):
            @pl.when(k == first_use)
            def _():
                w_loads[dt, 1].wait()
                w_loads[dt, 0].wait()

        for which, dst in ((0, cs), (1, mine)):
            dst[k, 800:, :] = jnp.zeros((KV_ROWS - 800, 2 * HD), BF16)
            weight = ws[dt_at * 2 + which]
            for lo, hi in ((0, cut), (cut, IMG_TOK)):
                dst[k, lo:hi, :] = jnp.dot(xs[img, lo:hi, :], weight, preferred_element_type=F32).astype(BF16)
            if which == 0:
                copy_of(kv_c[0] + k, cs.at[k], cr.at[k], "c").start()

        @pl.when(k > 0)
        def _():
            before = k - 1
            arrived(kv_c[0] + before, cr.at[before])
            mine[before] = (mine[before].astype(F32) + cr[before].astype(F32)).astype(BF16)

        return carry

    lax.fori_loop(0, 5, kv_slot, 0)

    half_tok = TOK // 2
    arrived(("tok", "y+"), tok.at[2])
    send(("tokf", "y+"), lambda: tok.at[2, 0:half_tok], lambda: tok.at[6, 0:half_tok], "y+")
    send(("tok", "c2"), lambda: tok.at[2], lambda: tok.at[4], "c")
    arrived(("tok", "y-"), tok.at[3])
    send(("tokf", "y-"), lambda: tok.at[3, half_tok:], lambda: tok.at[6, half_tok:], "y-")
    send(("tok", "c3"), lambda: tok.at[3], lambda: tok.at[5], "c")

    lax.fori_loop(5, 8, kv_slot, 0)

    send(("kv", "far", 0), lambda: mine.at[0], lambda: yr.at[0], "y+")
    send(("kv", "far", 1), lambda: mine.at[1], lambda: yr.at[1], "y-")
    arrived(kv_c[7], cr.at[7])
    mine[7] = (mine[7].astype(F32) + cr[7].astype(F32)).astype(BF16)

    arrived(("tok", "c0"), tok.at[1])
    arrived(("tok", "c2"), tok.at[4])
    arrived(("tok", "c3"), tok.at[5])
    acc[...] = jnp.zeros_like(acc)

    def project(n, carry):
        for m in range(8):
            @pl.when(n == m)
            def _():
                wq_loads[m].wait()

        rows = pl.ds(pl.multiple_of(n * width, width), width)
        acc[...] += jnp.dot(tok[n], wq[rows, :], preferred_element_type=F32)
        return carry

    lax.fori_loop(0, 6, project, 0)
    send(("kv", "near", 1, 1), lambda: mine.at[2], lambda: yr.at[3], "y+")
    send(("kv", "near", 3, 0), lambda: mine.at[3], lambda: yr.at[4], "y-")
    arrived(("tokf", "y+"), tok.at[6, 0:half_tok])
    arrived(("tokf", "y-"), tok.at[6, half_tok:])
    send(("tok", "c6"), lambda: tok.at[6], lambda: tok.at[7], "c")
    arrived(("tok", "c6"), tok.at[7])
    lax.fori_loop(6, 8, project, 0)

    eye = (
        lax.broadcasted_iota(jnp.int32, (HD, HD), 0) == lax.broadcasted_iota(jnp.int32, (HD, HD), 1)
    ).astype(F32)
    q_scale = qg_ref[...] * (math.log2(math.e) / math.sqrt(HD))
    for g in range(8):
        raw = acc[:, g * HD : (g + 1) * HD]
        inv = lax.rsqrt(jnp.mean(raw * raw, axis=-1, keepdims=True) + EPSILON)
        qall[cp, g // 4, (g % 4) * TOK : (g % 4 + 1) * TOK, :] = (raw * inv * q_scale).astype(BF16)
    eye_img = eye[:32, :32].astype(BF16)
    mask_rows = lax.dot_general(
        eye_img, mask_ref[...].astype(F32).astype(BF16), (((1,), (1,)), ((), ())), preferred_element_type=F32
    )
    for half in (0, 1):
        qall[cp, half, 512:, :] = mask_rows[half * 16 : (half + 1) * 16, :].astype(BF16)

    def shard(half, da, db):
        dx, dz = (da, db) if half == 0 else (db, da)
        return plus(x, dx) * RING + plus(z, dz)

    axes = (("x", "z"), ("z", "x"))
    lower, upper = pl.ds(0, CUT), pl.ds(CUT, HALF - CUT)

    def forward(tag, half, block, peer, rows=None):
        ref = lambda: qall.at[block, half] if rows is None else qall.at[block, half, rows]
        send(("q", half) + tag, ref, ref, peer)

    def q_arrived(tag, half, block, rows=None):
        ref = qall.at[block, half] if rows is None else qall.at[block, half, rows]
        arrived(("q", half) + tag, ref)

    for half in (0, 1):
        a, b = axes[half]
        forward(("a", 0), half, cp, a + "+")
        forward(("a", 1), half, cp, a + "-")
    for half in (0, 1):
        a, b = axes[half]
        forward(("b", 0, 0), half, cp, b + "+")
        forward(("b", 0, 1), half, cp, b + "-")

    arrived(("kv", "far", 0), yr.at[0])
    mine[4] = (mine[4].astype(F32) + yr[0].astype(F32)).astype(BF16)
    send(("kv", "near", 1, 0), lambda: mine.at[4], lambda: yr.at[2], "y+")
    arrived(("kv", "far", 1), yr.at[1])
    mine[5] = (mine[5].astype(F32) + yr[1].astype(F32)).astype(BF16)
    send(("kv", "near", 3, 1), lambda: mine.at[5], lambda: yr.at[5], "y-")

    for half in (0, 1):
        a, b = axes[half]
        q_arrived(("a", 0), half, shard(half, 3, 0))
        forward(("af", 0), half, shard(half, 3, 0), a + "+", lower)
        q_arrived(("a", 1), half, shard(half, 1, 0))
        forward(("af", 1), half, shard(half, 1, 0), a + "-", upper)
    for half in (0, 1):
        a, b = axes[half]
        for da in (3, 1):
            forward(("b", da, 0), half, shard(half, da, 0), b + "+")
            forward(("b", da, 1), half, shard(half, da, 0), b + "-")

    def pass_on(half, da):
        b = axes[half][1]
        q_arrived(("b", da, 0), half, shard(half, da, 3))
        forward(("bf", da, 0), half, shard(half, da, 3), b + "+", lower)
        q_arrived(("b", da, 1), half, shard(half, da, 1))
        forward(("bf", da, 1), half, shard(half, da, 1), b + "-", upper)

    for half in (0, 1):
        pass_on(half, 0)
    for half in (0, 1):
        a, b = axes[half]
        q_arrived(("af", 0), half, shard(half, 2, 0), lower)
        q_arrived(("af", 1), half, shard(half, 2, 0), upper)
        forward(("b", 2, 0), half, shard(half, 2, 0), b + "+")
        forward(("b", 2, 1), half, shard(half, 2, 0), b + "-")
    for da in (3, 1, 2):
        for half in (0, 1):
            pass_on(half, da)

    live = lax.broadcasted_iota(jnp.int32, (KV_ROWS, HD), 0) < IMG_TOK
    for img in (0, 1):
        kb[img, KV_ROWS:, :] = jnp.zeros((KEYS - KV_ROWS, HD), BF16)
        vb[img, KV_ROWS:, :] = jnp.zeros((KEYS - KV_ROWS, 2 * HD), BF16)
        vb[img, :KV_ROWS, HD:] = jnp.where(live, 1.0, 0.0).astype(BF16)
    for img in (1, 0):
        arrived(("kv", "near", 1, img), yr.at[2 + img])
        arrived(("kv", "near", 3, img), yr.at[4 + img])
        keys = (
            mine[6 + img, :, :HD].astype(F32) + yr[2 + img, :, :HD].astype(F32) + yr[4 + img, :, :HD].astype(F32)
        )
        inv = lax.rsqrt(jnp.mean(keys * keys, axis=-1, keepdims=True) + EPSILON)
        kb[img, :KV_ROWS, :] = jnp.where(live, keys * inv * kg_ref[...], 0.0).astype(BF16)
        values = (
            mine[6 + img, :, HD:].astype(F32) + yr[2 + img, :, HD:].astype(F32) + yr[4 + img, :, HD:].astype(F32)
        )
        vb[img, :KV_ROWS, :HD] = jnp.where(live, values, 0.0).astype(BF16)

    for da in (0, 3, 1, 2):
        for half in (0, 1):
            q_arrived(("bf", da, 0), half, shard(half, da, 2), lower)
            q_arrived(("bf", da, 1), half, shard(half, da, 2), upper)

    unit_of = {offset: u for u, offset in enumerate(UNITS)}
    rs_axes = (("z", "x"), ("x", "z"))

    def block(half, df, dg):
        return pb.at[half, unit_of[(dg, df) if half == 0 else (df, dg)]]

    def add_rows(ref, rows, other):
        ref[rows, :] = (ref[rows, :].astype(F32) + other[rows, :].astype(F32)).astype(BF16)

    def do(kind, half, dg):
        f, g = rs_axes[half]
        if kind == "far":
            ref, dst = lambda: block(half, 2, dg), lambda: rf.at[half, dg]
            send(("n", half, dg, "f0"), lambda: ref().at[lower], lambda: dst().at[lower], f + "+")
            send(("n", half, dg, "f1"), lambda: ref().at[upper], lambda: dst().at[upper], f + "-")
        elif kind == "up":
            arrived(("n", half, dg, "f0"), rf.at[half, dg, lower])
            add_rows(block(half, 1, dg), lower, rf.at[half, dg])
            send(("n", half, dg, "u"), lambda: block(half, 1, dg), lambda: rn.at[half, dg, 0], f + "+")
        elif kind == "down":
            arrived(("n", half, dg, "f1"), rf.at[half, dg, upper])
            add_rows(block(half, 3, dg), upper, rf.at[half, dg])
            send(("n", half, dg, "d"), lambda: block(half, 3, dg), lambda: rn.at[half, dg, 1], f + "-")
        elif kind == "total":
            arrived(("n", half, dg, "u"), rn.at[half, dg, 0])
            arrived(("n", half, dg, "d"), rn.at[half, dg, 1])
            ref = block(half, 0, dg)
            sums = ref[...].astype(F32) + rn[half, dg, 0].astype(F32) + rn[half, dg, 1].astype(F32)
            if dg == 0:
                total[half] = sums
            else:
                ref[...] = sums.astype(BF16)
        elif kind == "gfar":
            ref = lambda: block(half, 0, 2)
            send(("g", half, "f0"), lambda: ref().at[lower], lambda: rgf.at[half, lower], g + "+")
            send(("g", half, "f1"), lambda: ref().at[upper], lambda: rgf.at[half, upper], g + "-")
        elif kind == "gup":
            arrived(("g", half, "f0"), rgf.at[half, lower])
            add_rows(block(half, 0, 1), lower, rgf.at[half])
            send(("g", half, "u"), lambda: block(half, 0, 1), lambda: rgn.at[half, 0], g + "+")
        elif kind == "gdown":
            arrived(("g", half, "f1"), rgf.at[half, upper])
            add_rows(block(half, 0, 3), upper, rgf.at[half])
            send(("g", half, "d"), lambda: block(half, 0, 3), lambda: rgn.at[half, 1], g + "-")

    steps = lay_out(unit_of)
    doc_a, doc_b = doc_ref[2 * cp], doc_ref[2 * cp + 1]
    first_a, first_b = first_ref[doc_a], first_ref[doc_b]
    count_a, count_b = count_ref[doc_a], count_ref[doc_b]
    ones = jnp.ones((HD, HD), BF16)
    image_row = lax.broadcasted_iota(jnp.int32, (32, TOK), 0)
    on_a = (image_row == 2 * cp).astype(F32)
    on_b = (image_row == 2 * cp + 1).astype(F32)

    def unit(u, carry):
        j = plus(x, pick(u, [dx for dx, _ in UNITS])) * RING + plus(z, pick(u, [dz for _, dz in UNITS]))
        covers_a = ((first_a <= j) & (j < first_a + count_a)).astype(jnp.int32)
        covers_b = ((first_b <= j) & (j < first_b + count_b)).astype(jnp.int32)
        masks = jnp.concatenate([qall[j, 0, 512:, :], qall[j, 1, 512:, :]], axis=0).astype(F32)
        weigh = on_a * covers_a.astype(F32) + on_b * covers_b.astype(F32)
        weight_row = jnp.sum(masks * weigh, axis=0, keepdims=True)
        diagonal = eye * weight_row
        weight = jnp.dot(diagonal.astype(BF16), ones, preferred_element_type=F32)
        keys, values = kb[covers_b], vb[covers_b]
        for half in (0, 1):
            scores = lax.dot_general(
                qall[j, half, :512, :], keys, (((1,), (1,)), ((), ())), preferred_element_type=F32
            )
            probs = jnp.exp2(scores).astype(BF16)
            both = jnp.dot(probs, values, preferred_element_type=F32)
            denoms = []
            for g in range(4):
                rows = slice(g * TOK, (g + 1) * TOK)
                pb[half, u, rows, :] = (both[rows, :HD] * weight).astype(BF16)
                denoms.append(jnp.sum(both[rows, HD:] * diagonal, axis=0, keepdims=True))
            denoms.append(jnp.zeros((12, TOK), F32))
            pb[half, u, 512:, :] = jnp.concatenate(denoms, axis=0).astype(BF16)
        for at in range(len(UNITS)):
            here = [step for step in steps if step[0] == at]
            if here:
                @pl.when(u == at)
                def _():
                    for _, _, kind, half, dg in here:
                        do(kind, half, dg)
        return carry

    lax.fori_loop(0, len(UNITS), unit, 0)
    for slot, _, kind, half, dg in steps:
        if slot >= len(UNITS):
            do(kind, half, dg)

    for half in (0, 1):
        arrived(("g", half, "u"), rgn.at[half, 0])
        arrived(("g", half, "d"), rgn.at[half, 1])
        sums = total[half] + rgn[half, 0].astype(F32) + rgn[half, 1].astype(F32)
        for g in range(4):
            denom = sums[512 + g : 513 + g, :]
            inv = jnp.where(denom > 0, 1.0 / jnp.where(denom > 0, denom, 1.0), 0.0)
            inv = jnp.transpose(jnp.broadcast_to(inv, (TOK, TOK)))
            cols = slice((half * 4 + g) * HD, (half * 4 + g + 1) * HD)
            out_ref[:, cols] = (sums[g * TOK : (g + 1) * TOK, :] * inv).astype(BF16)

    for k in range(8):
        copy_of(kv_c[k], cs.at[k], cr.at[k], "c").wait_send()
    for key, src, dst, peer in started:
        copy_of(key, src(), dst(), peer).wait_send()


SEMAPHORES = 136


def per_device(
    image_rows, kv_weight, k_gain, tokens, ln_gain, q_weight, q_gain, image_doc, doc_first, doc_count, token_mask
):
    vmem = pl.BlockSpec(memory_space=pltpu.VMEM)
    smem = pl.BlockSpec(memory_space=pltpu.SMEM)
    hbm = pl.BlockSpec(memory_space=pl.ANY)
    width = kv_weight.shape[0]
    cols = q_weight.shape[1]
    scratch = [
        pltpu.VMEM(image_rows.shape, BF16),
        pltpu.VMEM((8, width, 2 * HD), BF16),
        pltpu.VMEM(q_weight.shape, BF16),
        pltpu.VMEM((8,) + tokens.shape, BF16),
        pltpu.VMEM((8, KV_ROWS, 2 * HD), BF16),
        pltpu.VMEM((8, KV_ROWS, 2 * HD), BF16),
        pltpu.VMEM((8, KV_ROWS, 2 * HD), BF16),
        pltpu.VMEM((6, KV_ROWS, 2 * HD), BF16),
        pltpu.VMEM((TOK, cols), F32),
        pltpu.VMEM((SHARDS, 2, HALF, HD), BF16),
        pltpu.VMEM((2, KEYS, HD), BF16),
        pltpu.VMEM((2, KEYS, 2 * HD), BF16),
        pltpu.VMEM((2, SHARDS, HALF, HD), BF16),
        pltpu.VMEM((2, RING, HALF, HD), BF16),
        pltpu.VMEM((2, RING, 2, HALF, HD), BF16),
        pltpu.VMEM((2, HALF, HD), BF16),
        pltpu.VMEM((2, 2, HALF, HD), BF16),
        pltpu.VMEM((2, HALF, HD), F32),
        pltpu.SemaphoreType.DMA((18,)),
        pltpu.SemaphoreType.DMA((SEMAPHORES,)),
        pltpu.SemaphoreType.DMA((SEMAPHORES,)),
    ]
    return pl.pallas_call(
        kernel,
        out_shape=jax.ShapeDtypeStruct((tokens.shape[0], cols), BF16),
        in_specs=[hbm, hbm, vmem, vmem, vmem, hbm, vmem, smem, smem, smem, vmem],
        out_specs=vmem,
        scratch_shapes=scratch,
        compiler_params=pltpu.CompilerParams(
            collective_id=0, has_side_effects=True, vmem_limit_bytes=62 * 2**20
        ),
        name="cross_attention",
    )(
        image_rows, kv_weight, k_gain.reshape(1, HD), tokens, ln_gain.reshape(8, 8, 128), q_weight,
        q_gain.reshape(1, HD), image_doc, doc_first, doc_count, token_mask,
    )


def solution(mesh):
    in_specs = (
        P("cp", None, ("segment", "tp")),
        P(("segment", "tp"), None),
        P(),
        P("cp", ("segment", "tp")),
        P(),
        P(None, ("segment", "tp")),
        P(),
        P(),
        P(),
        P(),
        P("cp", None),
    )
    out_specs = P("cp", ("segment", "tp"))
    return jax.shard_map(
        per_device, mesh=mesh, in_specs=in_specs, out_specs=out_specs, check_vma=False
    )
```

```python
import functools
import math

import jax
import jax.numpy as jnp
from jax import lax
from jax.experimental import pallas as pl
from jax.experimental.pallas import tpu as pltpu
from jax.sharding import PartitionSpec as P

EPSILON = 1e-06
MESH = pl.DeviceIdType.MESH
BF16 = jnp.bfloat16
F32 = jnp.float32

RING = 4
SHARDS = 16
TOK = 128
HD = 128
IMG_TOK = 801
KV_ROWS = 816
KV_CUT = 800
KV_ALL = 1632
KEYS = 896
HALF = 528
CUT = 256

KV_ORDER = ((2, 0), (2, 1), (1, 1), (3, 0), (1, 0), (3, 1), (0, 0), (0, 1))
UNITS = (
    (2, 2), (2, 1), (1, 2), (2, 3), (3, 2), (2, 0), (0, 2), (1, 1),
    (3, 3), (1, 3), (3, 1), (1, 0), (0, 1), (3, 0), (0, 3), (0, 0),
)
FAR_LAG = 3
NEAR_LAG = 5


def pick(index, values):
    return sum((index == at).astype(jnp.int32) * value for at, value in enumerate(values) if value)


def lay_out(unit_of):
    steps = []
    order = 0

    def add(slot, kind, half, dg):
        nonlocal order
        steps.append((slot, order, kind, half, dg))
        order += 1

    for half in (0, 1):
        unit = lambda df, dg: unit_of[(dg, df) if half == 0 else (df, dg)]
        total_at = {}
        for dg in (2, 1, 3, 0):
            far = unit(2, dg)
            add(far, "far", half, dg)
            up = max(unit(1, dg), far + FAR_LAG)
            down = max(unit(3, dg), far + FAR_LAG)
            add(up, "up", half, dg)
            add(down, "down", half, dg)
            total_at[dg] = max(unit(0, dg), max(up, down) + NEAR_LAG)
            add(total_at[dg], "total", half, dg)
        add(total_at[2], "gfar", half, 2)
        add(max(total_at[1], total_at[2] + FAR_LAG), "gup", half, 1)
        add(max(total_at[3], total_at[2] + FAR_LAG), "gdown", half, 3)
    return sorted(steps)


def kernel(
    x_hbm, w_hbm, kg_hbm, tok_hbm, ln_hbm, wq_hbm, qg_hbm, doc_hbm, first_hbm, count_hbm, mask_hbm,
    out_ref,
    kg_ref, tok_ref, ln_ref, qg_ref, doc_ref, first_ref, count_ref, mask_ref,
    x3, xs, ws, wq, tok, cs, cr, mine, yr, fk, fv, acc, qall, kb, vb, pb, rf, rn, rgf, rgn, total,
    load_sem, send_sem, recv_sem,
):
    s = lax.axis_index("segment")
    cp = lax.axis_index("cp")
    t = lax.axis_index("tp")
    x, z = cp // RING, cp % RING

    def plus(v, n):
        return lax.rem(v + n, RING)

    peers = {
        "c": (1 - s, cp, t),
        "y+": (s, cp, plus(t, 1)),
        "y-": (s, cp, plus(t, 3)),
        "x+": (s, plus(x, 1) * RING + z, t),
        "x-": (s, plus(x, 3) * RING + z, t),
        "z+": (s, x * RING + plus(z, 1), t),
        "z-": (s, x * RING + plus(z, 3), t),
    }

    numbers = {}

    def number(key):
        return numbers.setdefault(key, len(numbers))

    started = []

    def copy_of(key, src, dst, peer):
        n = number(key) if isinstance(key, tuple) else key
        return pltpu.make_async_remote_copy(
            src_ref=src, dst_ref=dst, send_sem=send_sem.at[n], recv_sem=recv_sem.at[n],
            device_id=peers[peer], device_id_type=MESH,
        )

    def send(key, src, dst, peer):
        copy_of(key, src(), dst(), peer).start()
        started.append((key, src, dst, peer))

    def arrived(key, dst):
        copy_of(key, dst, dst, "c").wait_recv()

    def load(n, src, dst):
        return pltpu.make_async_copy(src, dst, load_sem.at[n])

    def head_cols(head):
        return pl.ds(pl.multiple_of(head * 2 * HD, 2 * HD), 2 * HD)

    first_tok = 416
    x_loads = [
        load(0, x_hbm.at[pl.ds(0, first_tok)], x3.at[pl.ds(0, first_tok)]),
        load(1, x_hbm.at[pl.ds(first_tok, IMG_TOK - first_tok)], x3.at[pl.ds(first_tok, IMG_TOK - first_tok)]),
    ]
    w_loads = {}
    for at, dt in enumerate((2, 1, 3, 0)):
        for other in (1, 0):
            head = (1 - s if other else s) * RING + plus(t, dt)
            w_loads[dt, other] = load(
                2 + at * 2 + (1 - other), w_hbm.at[:, head_cols(head)], ws.at[at * 2 + (1 - other)]
            )
    tok_order = ((0, 0), (1, 0), (0, 3), (0, 1), (1, 3), (1, 1), (0, 2), (1, 2))
    blocks = [(1 - s if o else s) * RING + plus(t, dt) for o, dt in tok_order]
    width = wq.shape[0] // 8
    wq_loads = [
        load(10 + n, wq_hbm.at[pl.ds(pl.multiple_of(b * width, width), width)], wq.at[pl.ds(n * width, width)])
        for n, b in enumerate(blocks)
    ]
    small_loads = [
        load(18 + n, src, dst)
        for n, (src, dst) in enumerate(
            ((tok_hbm, tok_ref), (ln_hbm, ln_ref), (qg_hbm, qg_ref), (mask_hbm, mask_ref),
             (kg_hbm, kg_ref), (doc_hbm, doc_ref), (first_hbm, first_ref), (count_hbm, count_ref))
        )
    ]
    for copy in small_loads:
        copy.start()
    x_loads[0].start()
    w_loads[2, 1].start()
    w_loads[2, 0].start()
    x_loads[1].start()
    for dt in (1, 3, 0):
        w_loads[dt, 1].start()
        w_loads[dt, 0].start()

    barrier = pltpu.get_barrier_semaphore()
    for peer in peers.values():
        pl.semaphore_signal(barrier, inc=1, device_id=peer, device_id_type=MESH)

    small_loads[0].wait()
    small_loads[1].wait()
    gain = ln_ref[s * RING + t]
    for c in range(8):
        cols = slice(c * 128, (c + 1) * 128)
        tok[0, :, cols] = (tok_ref[:, cols].astype(F32) * gain[c : c + 1, :]).astype(BF16)
    for copy in small_loads[2:]:
        copy.wait()
    pl.semaphore_wait(barrier, len(peers))

    send(("tok", "y+"), lambda: tok.at[0], lambda: tok.at[2], "y+")
    send(("tok", "y-"), lambda: tok.at[0], lambda: tok.at[3], "y-")
    send(("tok", "c0"), lambda: tok.at[0], lambda: tok.at[1], "c")

    kv_c = [number(("kvc", k)) for k in range(8)]

    def interleave(lo, hi):
        def step(n, carry):
            rows = pl.ds(pl.multiple_of(n * 32, 32), 32)
            xs[rows, :] = x3[pl.ds(pl.multiple_of(n * 16, 16), 16)].reshape(32, x3.shape[2])
            return carry

        lax.fori_loop(lo, hi, step, 0)

    def kv_slot(k, carry):
        dt_at = pick(k, [(2, 1, 3, 0).index(dt) for dt, _ in KV_ORDER])
        half = pick(k, [h for _, h in KV_ORDER])

        @pl.when(k == 0)
        def _():
            x_loads[0].wait()
            interleave(0, first_tok // 16)
            w_loads[2, 1].wait()
            w_loads[2, 0].wait()

        @pl.when(k == 1)
        def _():
            x_loads[1].wait()
            for copy in wq_loads:
                copy.start()
            interleave(first_tok // 16, 50)
            last = x3[IMG_TOK - 1 : IMG_TOK].reshape(2, x3.shape[2])
            xs[2 * IMG_TOK - 2 :, :] = jnp.concatenate([last, jnp.zeros((14, x3.shape[2]), BF16)], axis=0)

        for first_use, dt in ((2, 1), (3, 3), (6, 0)):
            @pl.when(k == first_use)
            def _():
                w_loads[dt, 1].wait()
                w_loads[dt, 0].wait()

        rows = pl.ds(pl.multiple_of(half * KV_CUT, 32), KV_ROWS)
        for which, dst in ((0, cs), (1, mine)):
            dst[k] = jnp.dot(xs[rows, :], ws[dt_at * 2 + which], preferred_element_type=F32).astype(BF16)
            if which == 0:
                copy_of(kv_c[0] + k, cs.at[k], cr.at[k], "c").start()

        @pl.when(k > 1)
        def _():
            add_other(k - 2)

        return carry

    def add_other(k):
        arrived(kv_c[0] + k, cr.at[k])
        mine[k] = mine[k] + cr[k]

    halves = (pl.ds(0, KV_CUT), pl.ds(0, KV_ROWS))

    def send_kv(tag, k, to, peer):
        rows = halves[KV_ORDER[k][1]]
        send(("kv",) + tag, lambda: mine.at[k, rows], lambda: yr.at[to, rows], peer)

    def kv_arrived(tag, to, half):
        arrived(("kv",) + tag, yr.at[to, halves[half]])

    lax.fori_loop(0, 4, kv_slot, 0)

    half_tok = TOK // 2
    arrived(("tok", "y+"), tok.at[2])
    send(("tokf", "y+"), lambda: tok.at[2, 0:half_tok], lambda: tok.at[6, 0:half_tok], "y+")
    send(("tok", "c2"), lambda: tok.at[2], lambda: tok.at[4], "c")
    arrived(("tok", "y-"), tok.at[3])
    send(("tokf", "y-"), lambda: tok.at[3, half_tok:], lambda: tok.at[6, half_tok:], "y-")
    send(("tok", "c3"), lambda: tok.at[3], lambda: tok.at[5], "c")

    lax.fori_loop(4, 5, kv_slot, 0)
    send_kv(("far", 0), 0, 0, "y+")
    send_kv(("far", 1), 1, 1, "y-")

    arrived(("tok", "c0"), tok.at[1])
    arrived(("tok", "c2"), tok.at[4])
    arrived(("tok", "c3"), tok.at[5])
    acc[...] = jnp.zeros_like(acc)

    def project(n, carry):
        for m in range(8):
            @pl.when(n == m)
            def _():
                wq_loads[m].wait()

        rows = pl.ds(pl.multiple_of(n * width, width), width)
        acc[...] += jnp.dot(tok[n], wq[rows, :], preferred_element_type=F32)
        return carry

    lax.fori_loop(0, 6, project, 0)
    arrived(("tokf", "y+"), tok.at[6, 0:half_tok])
    arrived(("tokf", "y-"), tok.at[6, half_tok:])
    send(("tok", "c6"), lambda: tok.at[6], lambda: tok.at[7], "c")
    lax.fori_loop(5, 6, kv_slot, 0)
    send_kv(("near", 1, 1), 2, 3, "y+")
    send_kv(("near", 3, 0), 3, 4, "y-")
    arrived(("tok", "c6"), tok.at[7])
    lax.fori_loop(6, 8, project, 0)

    eye = (
        lax.broadcasted_iota(jnp.int32, (HD, HD), 0) == lax.broadcasted_iota(jnp.int32, (HD, HD), 1)
    ).astype(F32)
    q_scale = qg_ref[...] * (math.log2(math.e) / math.sqrt(HD))
    for g in range(8):
        raw = acc[:, g * HD : (g + 1) * HD]
        inv = lax.rsqrt(jnp.mean(raw * raw, axis=-1, keepdims=True) + EPSILON)
        qall[cp, g // 4, (g % 4) * TOK : (g % 4 + 1) * TOK, :] = (raw * inv * q_scale).astype(BF16)
    mask_rows = mask_ref[...].astype(F32)
    for half in (0, 1):
        qall[cp, half, 512:, :] = mask_rows[half * 16 : (half + 1) * 16, :].astype(BF16)

    def shard(half, da, db):
        dx, dz = (da, db) if half == 0 else (db, da)
        return plus(x, dx) * RING + plus(z, dz)

    axes = (("x", "z"), ("z", "x"))
    lower, upper = pl.ds(0, CUT), pl.ds(CUT, HALF - CUT)

    def forward(tag, half, block, peer, rows=None):
        ref = lambda: qall.at[block, half] if rows is None else qall.at[block, half, rows]
        send(("q", half) + tag, ref, ref, peer)

    def q_arrived(tag, half, block, rows=None):
        ref = qall.at[block, half] if rows is None else qall.at[block, half, rows]
        arrived(("q", half) + tag, ref)

    for half in (0, 1):
        a, b = axes[half]
        forward(("a", 0), half, cp, a + "+")
        forward(("a", 1), half, cp, a + "-")
    for half in (0, 1):
        a, b = axes[half]
        forward(("b", 0, 0), half, cp, b + "+")
        forward(("b", 0, 1), half, cp, b + "-")

    lax.fori_loop(6, 8, kv_slot, 0)
    add_other(6)
    add_other(7)

    def add_passing(k, to):
        rows = halves[KV_ORDER[k][1]]
        mine[k, rows, :] = mine[k, rows, :] + yr[to, rows, :]

    kv_arrived(("far", 0), 0, 0)
    add_passing(4, 0)
    send_kv(("near", 1, 0), 4, 2, "y+")
    kv_arrived(("far", 1), 1, 1)
    add_passing(5, 1)
    send_kv(("near", 3, 1), 5, 5, "y-")

    for half in (0, 1):
        a, b = axes[half]
        q_arrived(("a", 0), half, shard(half, 3, 0))
        forward(("af", 0), half, shard(half, 3, 0), a + "+", lower)
        q_arrived(("a", 1), half, shard(half, 1, 0))
        forward(("af", 1), half, shard(half, 1, 0), a + "-", upper)
    for half in (0, 1):
        a, b = axes[half]
        for da in (3, 1):
            forward(("b", da, 0), half, shard(half, da, 0), b + "+")
            forward(("b", da, 1), half, shard(half, da, 0), b + "-")

    def pass_on(half, da):
        b = axes[half][1]
        q_arrived(("b", da, 0), half, shard(half, da, 3))
        forward(("bf", da, 0), half, shard(half, da, 3), b + "+", lower)
        q_arrived(("b", da, 1), half, shard(half, da, 1))
        forward(("bf", da, 1), half, shard(half, da, 1), b + "-", upper)

    for half in (0, 1):
        pass_on(half, 0)
    for half in (0, 1):
        a, b = axes[half]
        q_arrived(("af", 0), half, shard(half, 2, 0), lower)
        q_arrived(("af", 1), half, shard(half, 2, 0), upper)
        forward(("b", 2, 0), half, shard(half, 2, 0), b + "+")
        forward(("b", 2, 1), half, shard(half, 2, 0), b + "-")
    for da in (3, 1, 2):
        for half in (0, 1):
            pass_on(half, da)

    live = lax.broadcasted_iota(jnp.int32, (KV_ROWS, HD), 0) < IMG_TOK
    for img in (0, 1):
        kb[img, KV_ROWS:, :] = jnp.zeros((KEYS - KV_ROWS, HD), BF16)
        vb[img, KV_ROWS:, :] = jnp.zeros((KEYS - KV_ROWS, 2 * HD), BF16)
        vb[img, :KV_ROWS, HD:] = jnp.where(live, 1.0, 0.0).astype(BF16)
    fk[KV_CUT + KV_ROWS :, :] = jnp.zeros((KV_ALL - KV_CUT - KV_ROWS, HD), F32)
    fv[KV_CUT + KV_ROWS :, :] = jnp.zeros((KV_ALL - KV_CUT - KV_ROWS, HD), F32)
    for half in (0, 1):
        kv_arrived(("near", 1, half), 2 + half, half)
        kv_arrived(("near", 3, half), 4 + half, half)
        rows = halves[half]
        to = pl.ds(half * KV_CUT, rows.size)
        for ref, cols in ((fk, slice(0, HD)), (fv, slice(HD, 2 * HD))):
            ref[to, :] = (
                mine[6 + half, rows, cols].astype(F32)
                + yr[2 + half, rows, cols].astype(F32)
                + yr[4 + half, rows, cols].astype(F32)
            )
    for img in (0, 1):
        every = pl.ds(img, KV_ROWS, stride=2)
        keys = fk[every, :]
        inv = lax.rsqrt(jnp.mean(keys * keys, axis=-1, keepdims=True) + EPSILON)
        kb[img, :KV_ROWS, :] = jnp.where(live, keys * inv * kg_ref[...], 0.0).astype(BF16)
        vb[img, :KV_ROWS, :HD] = jnp.where(live, fv[every, :], 0.0).astype(BF16)

    for da in (0, 3, 1, 2):
        for half in (0, 1):
            q_arrived(("bf", da, 0), half, shard(half, da, 2), lower)
            q_arrived(("bf", da, 1), half, shard(half, da, 2), upper)

    unit_of = {offset: u for u, offset in enumerate(UNITS)}
    rs_axes = (("z", "x"), ("x", "z"))

    def block(half, df, dg):
        return pb.at[half, unit_of[(dg, df) if half == 0 else (df, dg)]]

    def add_rows(ref, rows, other):
        ref[rows, :] = ref[rows, :] + other[rows, :]

    def do(kind, half, dg):
        f, g = rs_axes[half]
        if kind == "far":
            ref, dst = lambda: block(half, 2, dg), lambda: rf.at[half, dg]
            send(("n", half, dg, "f0"), lambda: ref().at[lower], lambda: dst().at[lower], f + "+")
            send(("n", half, dg, "f1"), lambda: ref().at[upper], lambda: dst().at[upper], f + "-")
        elif kind == "up":
            arrived(("n", half, dg, "f0"), rf.at[half, dg, lower])
            add_rows(block(half, 1, dg), lower, rf.at[half, dg])
            send(("n", half, dg, "u"), lambda: block(half, 1, dg), lambda: rn.at[half, dg, 0], f + "+")
        elif kind == "down":
            arrived(("n", half, dg, "f1"), rf.at[half, dg, upper])
            add_rows(block(half, 3, dg), upper, rf.at[half, dg])
            send(("n", half, dg, "d"), lambda: block(half, 3, dg), lambda: rn.at[half, dg, 1], f + "-")
        elif kind == "total":
            arrived(("n", half, dg, "u"), rn.at[half, dg, 0])
            arrived(("n", half, dg, "d"), rn.at[half, dg, 1])
            ref = block(half, 0, dg)
            sums = ref[...].astype(F32) + rn[half, dg, 0].astype(F32) + rn[half, dg, 1].astype(F32)
            if dg == 0:
                total[half] = sums
            else:
                ref[...] = sums.astype(BF16)
        elif kind == "gfar":
            ref = lambda: block(half, 0, 2)
            send(("g", half, "f0"), lambda: ref().at[lower], lambda: rgf.at[half, lower], g + "+")
            send(("g", half, "f1"), lambda: ref().at[upper], lambda: rgf.at[half, upper], g + "-")
        elif kind == "gup":
            arrived(("g", half, "f0"), rgf.at[half, lower])
            add_rows(block(half, 0, 1), lower, rgf.at[half])
            send(("g", half, "u"), lambda: block(half, 0, 1), lambda: rgn.at[half, 0], g + "+")
        elif kind == "gdown":
            arrived(("g", half, "f1"), rgf.at[half, upper])
            add_rows(block(half, 0, 3), upper, rgf.at[half])
            send(("g", half, "d"), lambda: block(half, 0, 3), lambda: rgn.at[half, 1], g + "-")

    steps = lay_out(unit_of)
    doc_a, doc_b = doc_ref[2 * cp], doc_ref[2 * cp + 1]
    first_a, first_b = first_ref[doc_a], first_ref[doc_b]
    count_a, count_b = count_ref[doc_a], count_ref[doc_b]
    ones = jnp.ones((HD, HD), BF16)
    image_row = lax.broadcasted_iota(jnp.int32, (32, TOK), 0)
    on_a = (image_row == 2 * cp).astype(F32)
    on_b = (image_row == 2 * cp + 1).astype(F32)

    def unit(u, carry):
        j = plus(x, pick(u, [dx for dx, _ in UNITS])) * RING + plus(z, pick(u, [dz for _, dz in UNITS]))
        covers_a = ((first_a <= j) & (j < first_a + count_a)).astype(jnp.int32)
        covers_b = ((first_b <= j) & (j < first_b + count_b)).astype(jnp.int32)
        masks = jnp.concatenate([qall[j, 0, 512:, :], qall[j, 1, 512:, :]], axis=0).astype(F32)
        weigh = on_a * covers_a.astype(F32) + on_b * covers_b.astype(F32)
        weight_row = jnp.sum(masks * weigh, axis=0, keepdims=True)
        diagonal = eye * weight_row
        weight = jnp.dot(diagonal.astype(BF16), ones, preferred_element_type=F32)
        keys, values = kb[covers_b], vb[covers_b]
        for half in (0, 1):
            scores = lax.dot_general(
                qall[j, half, :512, :], keys, (((1,), (1,)), ((), ())), preferred_element_type=F32
            )
            probs = jnp.exp2(scores).astype(BF16)
            both = jnp.dot(probs, values, preferred_element_type=F32)
            denoms = []
            for g in range(4):
                rows = slice(g * TOK, (g + 1) * TOK)
                pb[half, u, rows, :] = (both[rows, :HD] * weight).astype(BF16)
                denoms.append(jnp.sum(both[rows, HD:] * diagonal, axis=0, keepdims=True))
            denoms.append(jnp.zeros((12, TOK), F32))
            pb[half, u, 512:, :] = jnp.concatenate(denoms, axis=0).astype(BF16)
        for at in range(len(UNITS)):
            here = [step for step in steps if step[0] == at]
            if here:
                @pl.when(u == at)
                def _():
                    for _, _, kind, half, dg in here:
                        do(kind, half, dg)
        return carry

    lax.fori_loop(0, len(UNITS), unit, 0)
    for slot, _, kind, half, dg in steps:
        if slot >= len(UNITS):
            do(kind, half, dg)

    for half in (0, 1):
        arrived(("g", half, "u"), rgn.at[half, 0])
        arrived(("g", half, "d"), rgn.at[half, 1])
        sums = total[half] + rgn[half, 0].astype(F32) + rgn[half, 1].astype(F32)
        for g in range(4):
            denom = sums[512 + g : 513 + g, :]
            inv = jnp.where(denom > 0, 1.0 / jnp.where(denom > 0, denom, 1.0), 0.0)
            inv = jnp.transpose(jnp.broadcast_to(inv, (TOK, TOK)))
            cols = slice((half * 4 + g) * HD, (half * 4 + g + 1) * HD)
            out_ref[:, cols] = (sums[g * TOK : (g + 1) * TOK, :] * inv).astype(BF16)

    for k in range(8):
        copy_of(kv_c[k], cs.at[k], cr.at[k], "c").wait_send()
    for key, src, dst, peer in started:
        copy_of(key, src(), dst(), peer).wait_send()


SEMAPHORES = 136


def per_device(
    image_rows, kv_weight, k_gain, tokens, ln_gain, q_weight, q_gain, image_doc, doc_first, doc_count, token_mask
):
    vmem = pl.BlockSpec(memory_space=pltpu.VMEM)
    hbm = pl.BlockSpec(memory_space=pl.ANY)
    width = kv_weight.shape[0]
    cols = q_weight.shape[1]
    rows = jnp.transpose(image_rows, (1, 0, 2))
    scratch = [
        pltpu.VMEM((1, HD), F32),
        pltpu.VMEM(tokens.shape, BF16),
        pltpu.VMEM((8, 8, 128), F32),
        pltpu.VMEM((1, HD), F32),
        pltpu.SMEM(image_doc.shape, jnp.int32),
        pltpu.SMEM(doc_first.shape, jnp.int32),
        pltpu.SMEM(doc_count.shape, jnp.int32),
        pltpu.VMEM((32, TOK), jnp.int32),
        pltpu.VMEM(rows.shape, BF16),
        pltpu.VMEM((KV_CUT + KV_ROWS, width), BF16),
        pltpu.VMEM((8, width, 2 * HD), BF16),
        pltpu.VMEM(q_weight.shape, BF16),
        pltpu.VMEM((8,) + tokens.shape, BF16),
        pltpu.VMEM((8, KV_ROWS, 2 * HD), BF16),
        pltpu.VMEM((8, KV_ROWS, 2 * HD), BF16),
        pltpu.VMEM((8, KV_ROWS, 2 * HD), BF16),
        pltpu.VMEM((6, KV_ROWS, 2 * HD), BF16),
        pltpu.VMEM((KV_ALL, HD), F32),
        pltpu.VMEM((KV_ALL, HD), F32),
        pltpu.VMEM((TOK, cols), F32),
        pltpu.VMEM((SHARDS, 2, HALF, HD), BF16),
        pltpu.VMEM((2, KEYS, HD), BF16),
        pltpu.VMEM((2, KEYS, 2 * HD), BF16),
        pltpu.VMEM((2, SHARDS, HALF, HD), BF16),
        pltpu.VMEM((2, RING, HALF, HD), BF16),
        pltpu.VMEM((2, RING, 2, HALF, HD), BF16),
        pltpu.VMEM((2, HALF, HD), BF16),
        pltpu.VMEM((2, 2, HALF, HD), BF16),
        pltpu.VMEM((2, HALF, HD), F32),
        pltpu.SemaphoreType.DMA((26,)),
        pltpu.SemaphoreType.DMA((SEMAPHORES,)),
        pltpu.SemaphoreType.DMA((SEMAPHORES,)),
    ]
    return pl.pallas_call(
        kernel,
        out_shape=jax.ShapeDtypeStruct((tokens.shape[0], cols), BF16),
        in_specs=[hbm] * 11,
        out_specs=vmem,
        scratch_shapes=scratch,
        compiler_params=pltpu.CompilerParams(
            collective_id=0, has_side_effects=True, vmem_limit_bytes=62 * 2**20
        ),
        name="cross_attention",
    )(
        rows, kv_weight, k_gain.reshape(1, HD), tokens, ln_gain.reshape(8, 8, 128), q_weight,
        q_gain.reshape(1, HD), image_doc, doc_first, doc_count, token_mask.T,
    )


def solution(mesh):
    in_specs = (
        P("cp", None, ("segment", "tp")),
        P(("segment", "tp"), None),
        P(),
        P("cp", ("segment", "tp")),
        P(),
        P(None, ("segment", "tp")),
        P(),
        P(),
        P(),
        P(),
        P("cp", None),
    )
    out_specs = P("cp", ("segment", "tp"))
    return jax.shard_map(
        per_device, mesh=mesh, in_specs=in_specs, out_specs=out_specs, check_vma=False
    )
```

```python
import math

import jax
import jax.numpy as jnp
from jax import lax
from jax.experimental import pallas as pl
from jax.experimental.pallas import tpu as pltpu
from jax.sharding import PartitionSpec as P

EPSILON = 1e-06
MESH = pl.DeviceIdType.MESH
BF16 = jnp.bfloat16
F32 = jnp.float32

RING = 4
TOK = 128
HD = 128
IMG_TOK = 801
IMG_ROWS = 1616
KEYS = 896
HALF = 528


class Chunk:
    def __init__(self, key, keys, sent):
        self.key, self.keys = key, keys
        self.sent = sent
        self.row = 2 * key
        end = min(2 * (key + sent), IMG_ROWS)
        self.half = (end - self.row) // 32 * 16
        self.rows = end - self.row - self.half
        self.halves = (pl.ds(0, self.half), pl.ds(0, self.rows))


CHUNKS = (Chunk(0, 512, 512), Chunk(512, 384, 304))
KV_ORDER = ((2, 0), (2, 1), (1, 1), (3, 0), (1, 0), (3, 1), (0, 0), (0, 1))
SOURCES = (0, 3, 1, 2)
EARLY = 6
TARGETS = (2, 1, 3, 0)


def pick(index, values):
    return sum((index == at).astype(jnp.int32) * value for at, value in enumerate(values) if value)


def kernel(
    x_hbm, w_hbm, kg_hbm, tok_hbm, ln_hbm, wq_hbm, qg_hbm, doc_hbm, first_hbm, count_hbm, mask_hbm,
    out_ref,
    kg_ref, tok_ref, ln_ref, qg_ref, doc_ref, first_ref, count_ref, mask_ref,
    x3, xs, ws, wq, tok, fk, fv, acc, qall, weights, kvb, oacc, pb, rn,
    load_sem, send_sem, recv_sem,
    *kv_refs,
):
    s = lax.axis_index("segment")
    cp = lax.axis_index("cp")
    t = lax.axis_index("tp")
    x, z = cp // RING, cp % RING

    def plus(v, n):
        return lax.rem(v + n, RING)

    a, b = z * (1 - s) + x * s, x * (1 - s) + z * s

    def shard(da, db):
        at_a, at_b = plus(a, da), plus(b, db)
        return (at_b * (1 - s) + at_a * s) * RING + at_a * (1 - s) + at_b * s

    peers = {
        "c": (1 - s, cp, t),
        "y+": (s, cp, plus(t, 1)),
        "y-": (s, cp, plus(t, 3)),
        "a+": (s, shard(1, 0), t),
        "a-": (s, shard(3, 0), t),
        "b+": (s, shard(0, 1), t),
        "b-": (s, shard(0, 3), t),
        "a2": (s, shard(2, 0), t),
        "b2": (s, shard(0, 2), t),
    }

    numbers = {}

    def number(key):
        return numbers.setdefault(key, len(numbers))

    started = {}

    def copy_of(key, src, dst, peer):
        n = number(key) if isinstance(key, tuple) else key
        return pltpu.make_async_remote_copy(
            src_ref=src, dst_ref=dst, send_sem=send_sem.at[n], recv_sem=recv_sem.at[n],
            device_id=peers[peer], device_id_type=MESH,
        )

    def send(key, src, dst, peer):
        copy_of(key, src(), dst(), peer).start()
        started[key] = (src, dst, peer)

    def arrived(key, dst):
        copy_of(key, dst, dst, "c").wait_recv()

    def load(n, src, dst):
        return pltpu.make_async_copy(src, dst, load_sem.at[n])

    def head_cols(head):
        return pl.ds(pl.multiple_of(head * 2 * HD, 2 * HD), 2 * HD)

    first_tok = CHUNKS[0].sent
    x_loads = [
        load(0, x_hbm.at[pl.ds(0, first_tok)], x3.at[pl.ds(0, first_tok)]),
        load(1, x_hbm.at[pl.ds(first_tok, IMG_TOK - first_tok)], x3.at[pl.ds(first_tok, IMG_TOK - first_tok)]),
    ]
    w_loads = {}
    for at, dt in enumerate((2, 1, 3, 0)):
        for other in (1, 0):
            head = (1 - s if other else s) * RING + plus(t, dt)
            w_loads[dt, other] = load(
                2 + at * 2 + (1 - other), w_hbm.at[:, head_cols(head)], ws.at[at * 2 + (1 - other)]
            )
    tok_order = ((0, 0), (1, 0), (0, 3), (0, 1), (1, 3), (1, 1), (0, 2), (1, 2))
    blocks = [(1 - s if o else s) * RING + plus(t, dt) for o, dt in tok_order]
    width = wq.shape[0] // 8
    wq_loads = [
        load(10 + n, wq_hbm.at[pl.ds(pl.multiple_of(b * width, width), width)], wq.at[pl.ds(n * width, width)])
        for n, b in enumerate(blocks)
    ]
    small_loads = [
        load(18 + n, src, dst)
        for n, (src, dst) in enumerate(
            ((tok_hbm, tok_ref), (ln_hbm, ln_ref), (qg_hbm, qg_ref), (mask_hbm, mask_ref),
             (kg_hbm, kg_ref), (doc_hbm, doc_ref), (first_hbm, first_ref), (count_hbm, count_ref))
        )
    ]
    for copy in small_loads:
        copy.start()
    x_loads[0].start()
    w_loads[2, 1].start()
    w_loads[2, 0].start()
    x_loads[1].start()
    for dt in (1, 3, 0):
        w_loads[dt, 1].start()
        w_loads[dt, 0].start()

    barrier = pltpu.get_barrier_semaphore()
    for peer in peers.values():
        pl.semaphore_signal(barrier, inc=1, device_id=peer, device_id_type=MESH)

    small_loads[0].wait()
    small_loads[1].wait()
    gain = ln_ref[s * RING + t]
    for c in range(8):
        cols = slice(c * 128, (c + 1) * 128)
        tok[0, :, cols] = (tok_ref[:, cols].astype(F32) * gain[c : c + 1, :]).astype(BF16)
    for copy in small_loads[2:]:
        copy.wait()
    pl.semaphore_wait(barrier, len(peers))

    half_tok = TOK // 2
    tok_half = (slice(0, half_tok), slice(half_tok, TOK))

    def send_tok(tag, half, src, dst, peer):
        send(("tok",) + tag + (half,), lambda: tok.at[src, tok_half[half]], lambda: tok.at[dst, tok_half[half]], peer)

    def tok_arrived(tag, half, at):
        arrived(("tok",) + tag + (half,), tok.at[at, tok_half[half]])

    for first in (0, 1):
        send_tok(("y+",), first, 0, 2, "y+")
        send_tok(("y-",), 1 - first, 0, 3, "y-")
    send(("tok", "c0"), lambda: tok.at[0], lambda: tok.at[1], "c")

    n_chunks = len(CHUNKS)
    cs, cr, mine, yr = (kv_refs[n * n_chunks : (n + 1) * n_chunks] for n in range(4))
    kv_c = [[number(("kvc", c, k)) for k in range(8)][0] for c in range(n_chunks)]

    def interleave(lo, hi):
        def step(n, carry):
            rows = pl.ds(pl.multiple_of(n * 32, 32), 32)
            xs[rows, :] = x3[pl.ds(pl.multiple_of(n * 16, 16), 16)].reshape(32, x3.shape[2])
            return carry

        lax.fori_loop(lo, hi, step, 0)

    def kv_slots(c, which, lo, hi):
        chunk = CHUNKS[c]

        def kv_slot(k, carry):
            dt_at = pick(k, [(2, 1, 3, 0).index(dt) for dt, _ in KV_ORDER])
            half = pick(k, [h for _, h in KV_ORDER])
            for first_use, dt in ((0, 2), (2, 1), (3, 3), (6, 0)):
                if c == 0 and lo <= first_use < hi:
                    @pl.when(k == first_use)
                    def _():
                        w_loads[dt, 1 - which].wait()

            rows = pl.ds(pl.multiple_of(chunk.row + half * chunk.half, 16), chunk.rows)
            part = jnp.dot(xs[rows, :], ws[dt_at * 2 + which], preferred_element_type=F32).astype(BF16)
            if which == 0:
                cs[c][k] = part
                copy_of(kv_c[c] + k, cs[c].at[k], cr[c].at[k], "c").start()
            else:
                arrived(kv_c[c] + k, cr[c].at[k])
                mine[c][k] = part + cr[c][k]
            return carry

        lax.fori_loop(lo, hi, kv_slot, 0)

    OTHER, MINE = 0, 1

    def send_kv(c, tag, k, to, peer):
        rows = CHUNKS[c].halves[KV_ORDER[k][1]]
        send(("kv", c) + tag, lambda: mine[c].at[k, rows], lambda: yr[c].at[to, rows], peer)

    def kv_arrived(c, tag, to, half):
        arrived(("kv", c) + tag, yr[c].at[to, CHUNKS[c].halves[half]])

    def kv_far(c):
        send_kv(c, ("far", 0), 0, 0, "y+")
        send_kv(c, ("far", 1), 1, 1, "y-")

    def kv_near(c):
        send_kv(c, ("near", 1, 1), 2, 3, "y+")
        send_kv(c, ("near", 3, 0), 3, 4, "y-")

    def kv_pass(c):
        for half, k, tag, peer in ((0, 4, ("near", 1, 0), "y+"), (1, 5, ("near", 3, 1), "y-")):
            rows = CHUNKS[c].halves[half]
            kv_arrived(c, ("far", half), half, half)
            mine[c][k, rows, :] = mine[c][k, rows, :] + yr[c][half, rows, :]
            send_kv(c, tag, k, 2 if half == 0 else 5, peer)

    x_loads[0].wait()
    interleave(0, first_tok // 16)
    kv_slots(0, OTHER, 0, 6)
    x_loads[1].wait()
    for copy in wq_loads:
        copy.start()
    kv_slots(0, MINE, 0, 6)

    tok_arrived(("y+",), 0, 2)
    send_tok(("f+",), 0, 2, 6, "y+")
    tok_arrived(("y-",), 1, 3)
    send_tok(("f-",), 1, 3, 6, "y-")
    tok_arrived(("y+",), 1, 2)
    send(("tok", "c2"), lambda: tok.at[2], lambda: tok.at[4], "c")
    tok_arrived(("y-",), 0, 3)
    send(("tok", "c3"), lambda: tok.at[3], lambda: tok.at[5], "c")
    kv_far(0)

    kv_slots(0, OTHER, 6, 8)
    interleave(first_tok // 16, 50)
    last = x3[IMG_TOK - 1 : IMG_TOK].reshape(2, x3.shape[2])
    xs[2 * IMG_TOK - 2 :, :] = jnp.concatenate([last, jnp.zeros((IMG_ROWS - 2 * IMG_TOK, x3.shape[2]), BF16)], axis=0)
    for c in range(1, n_chunks):
        kv_slots(c, OTHER, 0, 8)

    arrived(("tok", "c0"), tok.at[1])
    arrived(("tok", "c2"), tok.at[4])
    arrived(("tok", "c3"), tok.at[5])
    acc[...] = jnp.zeros_like(acc)

    def project(n, carry):
        for m in range(8):
            @pl.when(n == m)
            def _():
                wq_loads[m].wait()

        rows = pl.ds(pl.multiple_of(n * width, width), width)
        acc[...] += jnp.dot(tok[n], wq[rows, :], preferred_element_type=F32)
        return carry

    lax.fori_loop(0, 6, project, 0)
    kv_near(0)
    tok_arrived(("f+",), 0, 6)
    send_tok(("c6",), 0, 6, 7, "c")
    tok_arrived(("f-",), 1, 6)
    send_tok(("c6",), 1, 6, 7, "c")
    kv_slots(1, MINE, 0, 6)
    tok_arrived(("c6",), 0, 7)
    tok_arrived(("c6",), 1, 7)
    lax.fori_loop(6, 8, project, 0)

    eye = (
        lax.broadcasted_iota(jnp.int32, (HD, HD), 0) == lax.broadcasted_iota(jnp.int32, (HD, HD), 1)
    ).astype(F32)
    q_scale = qg_ref[...] * (math.log2(math.e) / math.sqrt(HD))
    for g in range(8):
        raw = acc[:, g * HD : (g + 1) * HD]
        inv = lax.rsqrt(jnp.mean(raw * raw, axis=-1, keepdims=True) + EPSILON)
        qall[0, g // 4, (g % 4) * TOK : (g % 4 + 1) * TOK, :] = (raw * inv * q_scale).astype(BF16)
    mask_rows = mask_ref[...].astype(F32)
    for half in (0, 1):
        qall[0, half, 512:, :] = mask_rows[half * 16 : (half + 1) * 16, :].astype(BF16)

    ways = (("+", 3), ("-", 1), ("2", 2))
    for way, at in ways:
        send(("q", way), lambda: qall.at[0], lambda at=at: qall.at[at], "b" + way)

    kv_slots(0, MINE, 6, 8)
    kv_pass(0)
    kv_far(1)
    kv_near(1)
    kv_slots(1, MINE, 6, 8)

    tail = CHUNKS[-1].key + CHUNKS[-1].sent
    kvb[:, :, tail:, :] = jnp.zeros((RING, 2, KEYS - tail, 3 * HD), BF16)
    for chunk in CHUNKS:
        index = chunk.key + lax.broadcasted_iota(jnp.int32, (chunk.sent, HD), 0)
        ones_rows = jnp.where(index < IMG_TOK, 1.0, 0.0).astype(BF16)
        for da in range(RING):
            for img in (0, 1):
                kvb[da, img, chunk.key : chunk.key + chunk.sent, 2 * HD :] = ones_rows
    oacc[...] = jnp.zeros_like(oacc)
    fk[IMG_ROWS:, :] = jnp.zeros((16, HD), F32)
    fv[IMG_ROWS:, :] = jnp.zeros((16, HD), F32)

    def kv_ref(c, da):
        return kvb.at[da, :, pl.ds(CHUNKS[c].key, CHUNKS[c].sent), 0 : 2 * HD]

    def kv_finish(c):
        chunk = CHUNKS[c]
        for half in (0, 1):
            kv_arrived(c, ("near", 1, half), 2 + half, half)
            kv_arrived(c, ("near", 3, half), 4 + half, half)
            rows = chunk.halves[half]
            to = pl.ds(chunk.row + half * chunk.half, rows.size)
            for ref, cols in ((fk, slice(0, HD)), (fv, slice(HD, 2 * HD))):
                ref[to, :] = (
                    mine[c][6 + half, rows, cols].astype(F32)
                    + yr[c][2 + half, rows, cols].astype(F32)
                    + yr[c][4 + half, rows, cols].astype(F32)
                )
        live = chunk.key + lax.broadcasted_iota(jnp.int32, (chunk.sent, HD), 0) < IMG_TOK
        for img in (0, 1):
            every = pl.ds(chunk.row + img, chunk.sent, stride=2)
            rows = slice(chunk.key, chunk.key + chunk.sent)
            keys = fk[every, :]
            inv = lax.rsqrt(jnp.mean(keys * keys, axis=-1, keepdims=True) + EPSILON)
            kvb[0, img, rows, 0:HD] = jnp.where(live, keys * inv * kg_ref[...], 0.0).astype(BF16)
            kvb[0, img, rows, HD : 2 * HD] = jnp.where(live, fv[every, :], 0.0).astype(BF16)
        for way, at in ways[: 2 if c == 0 else 3]:
            send(("kva", c, way), lambda: kv_ref(c, 0), lambda at=at: kv_ref(c, at), "a" + way)

    def kv_gathered(c, way):
        at = dict(ways)[way]
        arrived(("kva", c, way), kv_ref(c, at))

    def kv_forward(img, way):
        at = dict(ways)[way]
        kv_gathered(0, way)
        send(("kvf", way), lambda: kv_ref(0, at).at[img], lambda: kv_ref(0, 2).at[img], "a" + way)

    def kv_forwarded():
        for img, way in ((0, "+"), (1, "-")):
            arrived(("kvf", way), kv_ref(0, 2).at[img])

    def settle(db):
        for half in (0, 1):
            pb[db, half, :512, :] = oacc[db, half * 512 : (half + 1) * 512, :HD].astype(BF16)
            denoms = [
                jnp.sum(oacc[db, half * 512 + g * TOK : half * 512 + (g + 1) * TOK, HD:] * eye, axis=0, keepdims=True)
                for g in range(4)
            ]
            pb[db, half, 512:, :] = jnp.concatenate(denoms + [jnp.zeros((12, TOK), F32)], axis=0).astype(BF16)

    def hand_over(db, way, at):
        settle(db)
        send(("n", way), lambda: pb.at[db], lambda: rn.at[at], "b" + way)

    ones = jnp.ones((HD, HD), BF16)
    image_row = lax.broadcasted_iota(jnp.int32, (32, TOK), 0)

    def covered(img, dst):
        doc = doc_ref[img]
        first = first_ref[doc]
        return ((first <= dst) & (dst < first + count_ref[doc])).astype(jnp.int32)

    def weigh(u, carry):
        da, db = lax.div(u, RING), lax.rem(u, RING)
        src, dst = shard(da, 0), shard(0, db)
        masks = jnp.concatenate([qall[db, 0, 512:, :], qall[db, 1, 512:, :]], axis=0).astype(F32)
        chosen = (image_row == 2 * src).astype(F32) * covered(2 * src, dst).astype(F32) + (
            image_row == 2 * src + 1
        ).astype(F32) * covered(2 * src + 1, dst).astype(F32)
        diagonal = eye * jnp.sum(masks * chosen, axis=0, keepdims=True)
        weights[da, db] = jnp.dot(diagonal.astype(BF16), ones, preferred_element_type=F32)
        return carry

    def attend(c, before, by_source):
        chunk = CHUNKS[c]
        rows = pl.ds(chunk.key, chunk.keys)

        def unit(u, carry):
            for at, events in before.items():
                @pl.when(u == at)
                def _():
                    for event in events:
                        event()
            outer, inner = lax.div(u, RING), lax.rem(u, RING)
            da, db = pick(outer if by_source else inner, SOURCES), pick(inner if by_source else outer, TARGETS)
            src, dst = shard(da, 0), shard(0, db)
            second = covered(2 * src + 1, dst)
            weight = weights[da, db]
            picked = jnp.where(second > 0, kvb[da, 1, rows, 0 : 2 * HD], kvb[da, 0, rows, 0 : 2 * HD])
            keys = picked[:, :HD]
            values = jnp.concatenate([picked[:, HD:], kvb[da, 0, rows, 2 * HD :]], axis=1)
            for half in (0, 1):
                scores = lax.dot_general(
                    qall[db, half, :512, :], keys, (((1,), (1,)), ((), ())), preferred_element_type=F32
                )
                both = jnp.dot(jnp.exp2(scores).astype(BF16), values, preferred_element_type=F32)
                for g in range(4):
                    to = slice(half * 512 + g * TOK, half * 512 + (g + 1) * TOK)
                    for cols in (slice(0, HD), slice(HD, 2 * HD)):
                        oacc[db, to, cols] += both[g * TOK : (g + 1) * TOK, cols] * weight
            return carry

        lax.fori_loop(0, RING * RING, unit, 0)

    for way, at in ways:
        arrived(("q", way), qall.at[at])
    lax.fori_loop(0, RING * RING, weigh, 0)
    kv_finish(0)
    attend(
        0,
        {
            3: [lambda: kv_pass(1)],
            4: [lambda: kv_forward(0, "+"), lambda: kv_forward(1, "-")],
            EARLY: [lambda: kv_finish(1)],
            12: [kv_forwarded],
        },
        True,
    )
    attend(
        1,
        {
            1: [lambda: kv_gathered(1, "+")],
            2: [lambda: kv_gathered(1, "-")],
            3: [lambda: kv_gathered(1, "2")],
            4: [lambda: hand_over(2, "2", 2)],
            8: [lambda: hand_over(1, "+", 0)],
            12: [lambda: hand_over(3, "-", 1)],
        },
        False,
    )

    for way, at in (("2", 2), ("+", 0), ("-", 1)):
        arrived(("n", way), rn.at[at])
    for half in (0, 1):
        for g in range(4):
            rows = slice(half * 512 + g * TOK, half * 512 + (g + 1) * TOK)
            at = slice(g * TOK, (g + 1) * TOK)
            denom = jnp.sum(oacc[0, rows, HD:] * eye, axis=0, keepdims=True)
            numer = oacc[0, rows, :HD]
            for n in range(3):
                denom += rn[n, half, 512 + g : 513 + g, :].astype(F32)
                numer += rn[n, half, at, :].astype(F32)
            inv = jnp.where(denom > 0, 1.0 / jnp.where(denom > 0, denom, 1.0), 0.0)
            inv = jnp.transpose(jnp.broadcast_to(inv, (TOK, TOK)))
            out_ref[:, (half * 4 + g) * HD : (half * 4 + g + 1) * HD] = (numer * inv).astype(BF16)

    for c in range(n_chunks):
        for k in range(8):
            copy_of(kv_c[c] + k, cs[c].at[k], cr[c].at[k], "c").wait_send()
    for key, (src, dst, peer) in started.items():
        copy_of(key, src(), dst(), peer).wait_send()


SEMAPHORES = 136


def per_device(
    image_rows, kv_weight, k_gain, tokens, ln_gain, q_weight, q_gain, image_doc, doc_first, doc_count, token_mask
):
    vmem = pl.BlockSpec(memory_space=pltpu.VMEM)
    hbm = pl.BlockSpec(memory_space=pl.ANY)
    width = kv_weight.shape[0]
    cols = q_weight.shape[1]
    rows = jnp.transpose(image_rows, (1, 0, 2))
    scratch = [
        pltpu.VMEM((1, HD), F32),
        pltpu.VMEM(tokens.shape, BF16),
        pltpu.VMEM((8, 8, 128), F32),
        pltpu.VMEM((1, HD), F32),
        pltpu.SMEM(image_doc.shape, jnp.int32),
        pltpu.SMEM(doc_first.shape, jnp.int32),
        pltpu.SMEM(doc_count.shape, jnp.int32),
        pltpu.VMEM((32, TOK), jnp.int32),
        pltpu.VMEM(rows.shape, BF16),
        pltpu.VMEM((IMG_ROWS, width), BF16),
        pltpu.VMEM((8, width, 2 * HD), BF16),
        pltpu.VMEM(q_weight.shape, BF16),
        pltpu.VMEM((8,) + tokens.shape, BF16),
        pltpu.VMEM((IMG_ROWS + 16, HD), F32),
        pltpu.VMEM((IMG_ROWS + 16, HD), F32),
        pltpu.VMEM((TOK, cols), F32),
        pltpu.VMEM((RING, 2, HALF, HD), BF16),
        pltpu.VMEM((RING, RING, TOK, HD), F32),
        pltpu.VMEM((RING, 2, KEYS, 3 * HD), BF16),
        pltpu.VMEM((RING, 8 * TOK, 2 * HD), F32),
        pltpu.VMEM((RING, 2, HALF, HD), BF16),
        pltpu.VMEM((3, 2, HALF, HD), BF16),
        pltpu.SemaphoreType.DMA((26,)),
        pltpu.SemaphoreType.DMA((SEMAPHORES,)),
        pltpu.SemaphoreType.DMA((SEMAPHORES,)),
        *[pltpu.VMEM((n, chunk.rows, 2 * HD), BF16) for n in (8, 8, 8, 6) for chunk in CHUNKS],
    ]
    return pl.pallas_call(
        kernel,
        out_shape=jax.ShapeDtypeStruct((tokens.shape[0], cols), BF16),
        in_specs=[hbm] * 11,
        out_specs=vmem,
        scratch_shapes=scratch,
        compiler_params=pltpu.CompilerParams(
            collective_id=0, has_side_effects=True, vmem_limit_bytes=62 * 2**20
        ),
        name="cross_attention",
    )(
        rows, kv_weight, k_gain.reshape(1, HD), tokens, ln_gain.reshape(8, 8, 128), q_weight,
        q_gain.reshape(1, HD), image_doc, doc_first, doc_count, token_mask.T,
    )


def solution(mesh):
    in_specs = (
        P("cp", None, ("segment", "tp")),
        P(("segment", "tp"), None),
        P(),
        P("cp", ("segment", "tp")),
        P(),
        P(None, ("segment", "tp")),
        P(),
        P(),
        P(),
        P(),
        P("cp", None),
    )
    out_specs = P("cp", ("segment", "tp"))
    return jax.shard_map(
        per_device, mesh=mesh, in_specs=in_specs, out_specs=out_specs, check_vma=False
    )
```

```python
import math

import jax
import jax.numpy as jnp
from jax import lax
from jax.experimental import pallas as pl
from jax.experimental.pallas import tpu as pltpu
from jax.sharding import PartitionSpec as P

EPSILON = 1e-06
MESH = pl.DeviceIdType.MESH
BF16 = jnp.bfloat16
F32 = jnp.float32

RING = 4
TOK = 128
HD = 128
IMG_TOK = 801
IMG_ROWS = 1616
KEYS = 896
HALF = 528


class Chunk:
    def __init__(self, key, keys, sent):
        self.key, self.keys = key, keys
        self.sent = sent
        self.row = 2 * key
        end = min(2 * (key + sent), IMG_ROWS)
        self.half = (end - self.row) // 32 * 16
        self.rows = end - self.row - self.half
        self.halves = (pl.ds(0, self.half), pl.ds(0, self.rows))


CHUNKS = (Chunk(0, 512, 512), Chunk(512, 384, 304))
KV_ORDER = ((2, 0), (2, 1), (1, 1), (3, 0), (1, 0), (3, 1), (0, 0), (0, 1))
SOURCES = (0, 3, 1, 2)
EARLY = 6
TARGETS = (2, 1, 3, 0)


def pick(index, values):
    return sum((index == at).astype(jnp.int32) * value for at, value in enumerate(values) if value)


def kernel(
    x_hbm, w_hbm, kg_hbm, tok_hbm, ln_hbm, wq_hbm, qg_hbm, doc_hbm, first_hbm, count_hbm, mask_hbm,
    out_ref,
    kg_ref, tok_ref, ln_ref, qg_ref, doc_ref, first_ref, count_ref, mask_ref,
    x3, xs, ws, wq, tok, fk, fv, acc, qall, weights, kvb, oacc, pb, rn,
    load_sem, send_sem, recv_sem,
    *kv_refs,
):
    s = lax.axis_index("segment")
    cp = lax.axis_index("cp")
    t = lax.axis_index("tp")
    x, z = cp // RING, cp % RING

    def plus(v, n):
        return lax.rem(v + n, RING)

    a, b = z * (1 - s) + x * s, x * (1 - s) + z * s

    def shard(da, db):
        at_a, at_b = plus(a, da), plus(b, db)
        return (at_b * (1 - s) + at_a * s) * RING + at_a * (1 - s) + at_b * s

    peers = {
        "c": (1 - s, cp, t),
        "y+": (s, cp, plus(t, 1)),
        "y-": (s, cp, plus(t, 3)),
        "a+": (s, shard(1, 0), t),
        "a-": (s, shard(3, 0), t),
        "b+": (s, shard(0, 1), t),
        "b-": (s, shard(0, 3), t),
        "a2": (s, shard(2, 0), t),
        "b2": (s, shard(0, 2), t),
    }

    numbers = {}

    def number(key):
        return numbers.setdefault(key, len(numbers))

    started = {}

    def copy_of(key, src, dst, peer):
        n = number(key) if isinstance(key, tuple) else key
        return pltpu.make_async_remote_copy(
            src_ref=src, dst_ref=dst, send_sem=send_sem.at[n], recv_sem=recv_sem.at[n],
            device_id=peers[peer], device_id_type=MESH,
        )

    def send(key, src, dst, peer):
        copy_of(key, src(), dst(), peer).start()
        started[key] = (src, dst, peer)

    def arrived(key, dst):
        copy_of(key, dst, dst, "c").wait_recv()

    def load(n, src, dst):
        return pltpu.make_async_copy(src, dst, load_sem.at[n])

    def head_cols(head):
        return pl.ds(pl.multiple_of(head * 2 * HD, 2 * HD), 2 * HD)

    first_tok = CHUNKS[0].sent
    x_loads = [
        load(0, x_hbm.at[pl.ds(0, first_tok)], x3.at[pl.ds(0, first_tok)]),
        load(1, x_hbm.at[pl.ds(first_tok, IMG_TOK - first_tok)], x3.at[pl.ds(first_tok, IMG_TOK - first_tok)]),
    ]
    w_loads = {}
    for at, dt in enumerate((2, 1, 3, 0)):
        for other in (1, 0):
            head = (1 - s if other else s) * RING + plus(t, dt)
            w_loads[dt, other] = load(
                2 + at * 2 + (1 - other), w_hbm.at[:, head_cols(head)], ws.at[at * 2 + (1 - other)]
            )
    tok_order = ((0, 0), (1, 0), (0, 3), (0, 1), (1, 3), (1, 1), (0, 2), (1, 2))
    blocks = [(1 - s if o else s) * RING + plus(t, dt) for o, dt in tok_order]
    width = wq.shape[0] // 8
    wq_loads = [
        load(10 + n, wq_hbm.at[pl.ds(pl.multiple_of(b * width, width), width)], wq.at[pl.ds(n * width, width)])
        for n, b in enumerate(blocks)
    ]
    small_loads = [
        load(18 + n, src, dst)
        for n, (src, dst) in enumerate(
            ((tok_hbm, tok_ref), (ln_hbm, ln_ref), (qg_hbm, qg_ref), (mask_hbm, mask_ref),
             (kg_hbm, kg_ref), (doc_hbm, doc_ref), (first_hbm, first_ref), (count_hbm, count_ref))
        )
    ]
    for copy in small_loads:
        copy.start()
    x_loads[0].start()
    w_loads[2, 1].start()
    w_loads[2, 0].start()
    x_loads[1].start()
    for dt in (1, 3, 0):
        w_loads[dt, 1].start()
        w_loads[dt, 0].start()

    barrier = pltpu.get_barrier_semaphore()
    for peer in peers.values():
        pl.semaphore_signal(barrier, inc=1, device_id=peer, device_id_type=MESH)

    small_loads[0].wait()
    small_loads[1].wait()
    gain = ln_ref[s * RING + t]
    for c in range(8):
        cols = slice(c * 128, (c + 1) * 128)
        tok[0, :, cols] = (tok_ref[:, cols].astype(F32) * gain[c : c + 1, :]).astype(BF16)
    for copy in small_loads[2:]:
        copy.wait()
    pl.semaphore_wait(barrier, len(peers))

    half_tok = TOK // 2
    tok_half = (slice(0, half_tok), slice(half_tok, TOK))

    def send_tok(tag, half, src, dst, peer):
        send(("tok",) + tag + (half,), lambda: tok.at[src, tok_half[half]], lambda: tok.at[dst, tok_half[half]], peer)

    def tok_arrived(tag, half, at):
        arrived(("tok",) + tag + (half,), tok.at[at, tok_half[half]])

    for first in (0, 1):
        send_tok(("y+",), first, 0, 2, "y+")
        send_tok(("y-",), 1 - first, 0, 3, "y-")
    send(("tok", "c0"), lambda: tok.at[0], lambda: tok.at[1], "c")

    n_chunks = len(CHUNKS)
    cs, cr, mine, yr = (kv_refs[n * n_chunks : (n + 1) * n_chunks] for n in range(4))
    kv_c = [[number(("kvc", c, k)) for k in range(8)][0] for c in range(n_chunks)]

    def interleave(lo, hi):
        def step(n, carry):
            rows = pl.ds(pl.multiple_of(n * 32, 32), 32)
            xs[rows, :] = x3[pl.ds(pl.multiple_of(n * 16, 16), 16)].reshape(32, x3.shape[2])
            return carry

        lax.fori_loop(lo, hi, step, 0)

    def kv_slots(c, which, lo, hi):
        chunk = CHUNKS[c]

        def kv_slot(k, carry):
            dt_at = pick(k, [(2, 1, 3, 0).index(dt) for dt, _ in KV_ORDER])
            half = pick(k, [h for _, h in KV_ORDER])
            for first_use, dt in ((0, 2), (2, 1), (3, 3), (6, 0)):
                if c == 0 and lo <= first_use < hi:
                    @pl.when(k == first_use)
                    def _():
                        w_loads[dt, 1 - which].wait()

            rows = pl.ds(pl.multiple_of(chunk.row + half * chunk.half, 16), chunk.rows)
            part = jnp.dot(xs[rows, :], ws[dt_at * 2 + which], preferred_element_type=F32).astype(BF16)
            if which == 0:
                cs[c][k] = part
                copy_of(kv_c[c] + k, cs[c].at[k], cr[c].at[k], "c").start()
            else:
                arrived(kv_c[c] + k, cr[c].at[k])
                mine[c][k] = part + cr[c][k]
            return carry

        lax.fori_loop(lo, hi, kv_slot, 0)

    OTHER, MINE = 0, 1

    def send_kv(c, tag, k, to, peer):
        rows = CHUNKS[c].halves[KV_ORDER[k][1]]
        send(("kv", c) + tag, lambda: mine[c].at[k, rows], lambda: yr[c].at[to, rows], peer)

    def kv_arrived(c, tag, to, half):
        arrived(("kv", c) + tag, yr[c].at[to, CHUNKS[c].halves[half]])

    def kv_far(c):
        send_kv(c, ("far", 0), 0, 0, "y+")
        send_kv(c, ("far", 1), 1, 1, "y-")

    def kv_near(c):
        send_kv(c, ("near", 1, 1), 2, 3, "y+")
        send_kv(c, ("near", 3, 0), 3, 4, "y-")

    def kv_pass(c):
        for half, k, tag, peer in ((0, 4, ("near", 1, 0), "y+"), (1, 5, ("near", 3, 1), "y-")):
            rows = CHUNKS[c].halves[half]
            kv_arrived(c, ("far", half), half, half)
            mine[c][k, rows, :] = mine[c][k, rows, :] + yr[c][half, rows, :]
            send_kv(c, tag, k, 2 if half == 0 else 5, peer)

    x_loads[0].wait()
    interleave(0, first_tok // 16)
    kv_slots(0, OTHER, 0, 6)
    x_loads[1].wait()
    for copy in wq_loads:
        copy.start()
    kv_slots(0, MINE, 0, 6)

    tok_arrived(("y+",), 0, 2)
    send_tok(("f+",), 0, 2, 6, "y+")
    tok_arrived(("y-",), 1, 3)
    send_tok(("f-",), 1, 3, 6, "y-")
    tok_arrived(("y+",), 1, 2)
    send(("tok", "c2"), lambda: tok.at[2], lambda: tok.at[4], "c")
    tok_arrived(("y-",), 0, 3)
    send(("tok", "c3"), lambda: tok.at[3], lambda: tok.at[5], "c")
    kv_far(0)

    kv_slots(0, OTHER, 6, 8)
    interleave(first_tok // 16, 50)
    last = x3[IMG_TOK - 1 : IMG_TOK].reshape(2, x3.shape[2])
    xs[2 * IMG_TOK - 2 :, :] = jnp.concatenate([last, jnp.zeros((IMG_ROWS - 2 * IMG_TOK, x3.shape[2]), BF16)], axis=0)
    for c in range(1, n_chunks):
        kv_slots(c, OTHER, 0, 8)

    arrived(("tok", "c0"), tok.at[1])
    arrived(("tok", "c2"), tok.at[4])
    arrived(("tok", "c3"), tok.at[5])
    acc[...] = jnp.zeros_like(acc)

    def project(n, carry):
        for m in range(8):
            @pl.when(n == m)
            def _():
                wq_loads[m].wait()

        rows = pl.ds(pl.multiple_of(n * width, width), width)
        acc[...] += jnp.dot(tok[n], wq[rows, :], preferred_element_type=F32)
        return carry

    lax.fori_loop(0, 6, project, 0)
    kv_near(0)
    tok_arrived(("f+",), 0, 6)
    send_tok(("c6",), 0, 6, 7, "c")
    tok_arrived(("f-",), 1, 6)
    send_tok(("c6",), 1, 6, 7, "c")
    kv_slots(1, MINE, 0, 6)
    tok_arrived(("c6",), 0, 7)
    tok_arrived(("c6",), 1, 7)
    lax.fori_loop(6, 8, project, 0)

    eye = (
        lax.broadcasted_iota(jnp.int32, (HD, HD), 0) == lax.broadcasted_iota(jnp.int32, (HD, HD), 1)
    ).astype(F32)
    q_scale = qg_ref[...] * (math.log2(math.e) / math.sqrt(HD))
    for g in range(8):
        raw = acc[:, g * HD : (g + 1) * HD]
        inv = lax.rsqrt(jnp.mean(raw * raw, axis=-1, keepdims=True) + EPSILON)
        qall[0, g // 4, (g % 4) * TOK : (g % 4 + 1) * TOK, :] = (raw * inv * q_scale).astype(BF16)
    mask_rows = mask_ref[...].astype(F32)
    for half in (0, 1):
        qall[0, half, 512:, :] = mask_rows[half * 16 : (half + 1) * 16, :].astype(BF16)

    ways = (("+", 3), ("-", 1), ("2", 2))
    for way, at in ways:
        send(("q", way), lambda: qall.at[0], lambda at=at: qall.at[at], "b" + way)

    kv_slots(0, MINE, 6, 8)
    kv_pass(0)
    kv_far(1)
    kv_near(1)
    kv_slots(1, MINE, 6, 8)

    tail = CHUNKS[-1].key + CHUNKS[-1].sent
    kvb[:, :, tail:, :] = jnp.zeros((RING, 2, KEYS - tail, 3 * HD), BF16)
    for chunk in CHUNKS:
        index = chunk.key + lax.broadcasted_iota(jnp.int32, (chunk.sent, HD), 0)
        ones_rows = jnp.where(index < IMG_TOK, 1.0, 0.0).astype(BF16)
        for da in range(RING):
            for img in (0, 1):
                kvb[da, img, chunk.key : chunk.key + chunk.sent, 2 * HD :] = ones_rows
    oacc[...] = jnp.zeros_like(oacc)
    fk[IMG_ROWS:, :] = jnp.zeros((16, HD), F32)
    fv[IMG_ROWS:, :] = jnp.zeros((16, HD), F32)

    def kv_ref(c, da):
        return kvb.at[da, :, pl.ds(CHUNKS[c].key, CHUNKS[c].sent), 0 : 2 * HD]

    def kv_finish(c):
        chunk = CHUNKS[c]
        for half in (0, 1):
            kv_arrived(c, ("near", 1, half), 2 + half, half)
            kv_arrived(c, ("near", 3, half), 4 + half, half)
            rows = chunk.halves[half]
            to = pl.ds(chunk.row + half * chunk.half, rows.size)
            for ref, cols in ((fk, slice(0, HD)), (fv, slice(HD, 2 * HD))):
                ref[to, :] = (
                    mine[c][6 + half, rows, cols].astype(F32)
                    + yr[c][2 + half, rows, cols].astype(F32)
                    + yr[c][4 + half, rows, cols].astype(F32)
                )
        live = chunk.key + lax.broadcasted_iota(jnp.int32, (chunk.sent, HD), 0) < IMG_TOK
        for img in (0, 1):
            every = pl.ds(chunk.row + img, chunk.sent, stride=2)
            rows = slice(chunk.key, chunk.key + chunk.sent)
            keys = fk[every, :]
            inv = lax.rsqrt(jnp.mean(keys * keys, axis=-1, keepdims=True) + EPSILON)
            kvb[0, img, rows, 0:HD] = jnp.where(live, keys * inv * kg_ref[...], 0.0).astype(BF16)
            kvb[0, img, rows, HD : 2 * HD] = jnp.where(live, fv[every, :], 0.0).astype(BF16)
        for way, at in ways[: 2 if c == 0 else 3]:
            send(("kva", c, way), lambda: kv_ref(c, 0), lambda at=at: kv_ref(c, at), "a" + way)

    def kv_gathered(c, way):
        at = dict(ways)[way]
        arrived(("kva", c, way), kv_ref(c, at))

    def kv_forward(img, way):
        at = dict(ways)[way]
        kv_gathered(0, way)
        send(("kvf", way), lambda: kv_ref(0, at).at[img], lambda: kv_ref(0, 2).at[img], "a" + way)

    def kv_forwarded():
        for img, way in ((0, "+"), (1, "-")):
            arrived(("kvf", way), kv_ref(0, 2).at[img])

    def settle(db):
        for half in (0, 1):
            pb[db, half, :512, :] = oacc[db, half * 512 : (half + 1) * 512, :HD].astype(BF16)
            denoms = [
                jnp.sum(oacc[db, half * 512 + g * TOK : half * 512 + (g + 1) * TOK, HD:] * eye, axis=0, keepdims=True)
                for g in range(4)
            ]
            pb[db, half, 512:, :] = jnp.concatenate(denoms + [jnp.zeros((12, TOK), F32)], axis=0).astype(BF16)

    def hand_over(db, way, at):
        settle(db)
        send(("n", way), lambda: pb.at[db], lambda: rn.at[at], "b" + way)

    ones = jnp.ones((HD, HD), BF16)
    image_row = lax.broadcasted_iota(jnp.int32, (32, TOK), 0)

    def covered(img, dst):
        doc = doc_ref[img]
        first = first_ref[doc]
        return ((first <= dst) & (dst < first + count_ref[doc])).astype(jnp.int32)

    def weigh(u, carry):
        da, db = lax.div(u, RING), lax.rem(u, RING)
        src, dst = shard(da, 0), shard(0, db)
        masks = jnp.concatenate([qall[db, 0, 512:, :], qall[db, 1, 512:, :]], axis=0).astype(F32)
        chosen = (image_row == 2 * src).astype(F32) * covered(2 * src, dst).astype(F32) + (
            image_row == 2 * src + 1
        ).astype(F32) * covered(2 * src + 1, dst).astype(F32)
        diagonal = eye * jnp.sum(masks * chosen, axis=0, keepdims=True)
        weights[da, db] = jnp.dot(diagonal.astype(BF16), ones, preferred_element_type=F32)
        return carry

    def attend(c, before, by_source):
        chunk = CHUNKS[c]
        rows = pl.ds(chunk.key, chunk.keys)

        def units(step, carry):
            for at, events in before.items():
                @pl.when(step * 2 == at)
                def _():
                    for event in events:
                        event()
            for u in (step * 2, step * 2 + 1):
                outer, inner = lax.div(u, RING), lax.rem(u, RING)
                da, db = pick(outer if by_source else inner, SOURCES), pick(inner if by_source else outer, TARGETS)
                second = covered(2 * shard(da, 0) + 1, shard(0, db))
                weight = weights[da, db]
                picked = jnp.where(second > 0, kvb[da, 1, rows, 0 : 2 * HD], kvb[da, 0, rows, 0 : 2 * HD])
                keys = picked[:, :HD]
                values = jnp.concatenate([picked[:, HD:], kvb[da, 0, rows, 2 * HD :]], axis=1)
                for half in (0, 1):
                    scores = lax.dot_general(
                        qall[db, half, :512, :], keys, (((1,), (1,)), ((), ())), preferred_element_type=F32
                    )
                    both = jnp.dot(jnp.exp2(scores).astype(BF16), values, preferred_element_type=F32)
                    for g in range(4):
                        to = slice(half * 512 + g * TOK, half * 512 + (g + 1) * TOK)
                        for cols in (slice(0, HD), slice(HD, 2 * HD)):
                            oacc[db, to, cols] += both[g * TOK : (g + 1) * TOK, cols] * weight
            return carry

        lax.fori_loop(0, RING * RING // 2, units, 0)

    for way, at in ways:
        arrived(("q", way), qall.at[at])
    lax.fori_loop(0, RING * RING, weigh, 0)
    kv_finish(0)
    attend(
        0,
        {
            2: [lambda: kv_pass(1)],
            4: [lambda: kv_forward(0, "+"), lambda: kv_forward(1, "-")],
            EARLY: [lambda: kv_finish(1)],
            12: [kv_forwarded],
        },
        True,
    )
    attend(
        1,
        {
            0: [lambda: kv_gathered(1, "+")],
            2: [lambda: kv_gathered(1, "-"), lambda: kv_gathered(1, "2")],
            4: [lambda: hand_over(2, "2", 2)],
            8: [lambda: hand_over(1, "+", 0)],
            12: [lambda: hand_over(3, "-", 1)],
        },
        False,
    )

    for way, at in (("2", 2), ("+", 0), ("-", 1)):
        arrived(("n", way), rn.at[at])
    for half in (0, 1):
        for g in range(4):
            rows = slice(half * 512 + g * TOK, half * 512 + (g + 1) * TOK)
            at = slice(g * TOK, (g + 1) * TOK)
            denom = jnp.sum(oacc[0, rows, HD:] * eye, axis=0, keepdims=True)
            numer = oacc[0, rows, :HD]
            for n in range(3):
                denom += rn[n, half, 512 + g : 513 + g, :].astype(F32)
                numer += rn[n, half, at, :].astype(F32)
            inv = jnp.where(denom > 0, 1.0 / jnp.where(denom > 0, denom, 1.0), 0.0)
            inv = jnp.transpose(jnp.broadcast_to(inv, (TOK, TOK)))
            out_ref[:, (half * 4 + g) * HD : (half * 4 + g + 1) * HD] = (numer * inv).astype(BF16)

    for c in range(n_chunks):
        for k in range(8):
            copy_of(kv_c[c] + k, cs[c].at[k], cr[c].at[k], "c").wait_send()
    for key, (src, dst, peer) in started.items():
        copy_of(key, src(), dst(), peer).wait_send()


SEMAPHORES = 136


def per_device(
    image_rows, kv_weight, k_gain, tokens, ln_gain, q_weight, q_gain, image_doc, doc_first, doc_count, token_mask
):
    vmem = pl.BlockSpec(memory_space=pltpu.VMEM)
    hbm = pl.BlockSpec(memory_space=pl.ANY)
    width = kv_weight.shape[0]
    cols = q_weight.shape[1]
    rows = jnp.transpose(image_rows, (1, 0, 2))
    scratch = [
        pltpu.VMEM((1, HD), F32),
        pltpu.VMEM(tokens.shape, BF16),
        pltpu.VMEM((8, 8, 128), F32),
        pltpu.VMEM((1, HD), F32),
        pltpu.SMEM(image_doc.shape, jnp.int32),
        pltpu.SMEM(doc_first.shape, jnp.int32),
        pltpu.SMEM(doc_count.shape, jnp.int32),
        pltpu.VMEM((32, TOK), jnp.int32),
        pltpu.VMEM(rows.shape, BF16),
        pltpu.VMEM((IMG_ROWS, width), BF16),
        pltpu.VMEM((8, width, 2 * HD), BF16),
        pltpu.VMEM(q_weight.shape, BF16),
        pltpu.VMEM((8,) + tokens.shape, BF16),
        pltpu.VMEM((IMG_ROWS + 16, HD), F32),
        pltpu.VMEM((IMG_ROWS + 16, HD), F32),
        pltpu.VMEM((TOK, cols), F32),
        pltpu.VMEM((RING, 2, HALF, HD), BF16),
        pltpu.VMEM((RING, RING, TOK, HD), F32),
        pltpu.VMEM((RING, 2, KEYS, 3 * HD), BF16),
        pltpu.VMEM((RING, 8 * TOK, 2 * HD), F32),
        pltpu.VMEM((RING, 2, HALF, HD), BF16),
        pltpu.VMEM((3, 2, HALF, HD), BF16),
        pltpu.SemaphoreType.DMA((26,)),
        pltpu.SemaphoreType.DMA((SEMAPHORES,)),
        pltpu.SemaphoreType.DMA((SEMAPHORES,)),
        *[pltpu.VMEM((n, chunk.rows, 2 * HD), BF16) for n in (8, 8, 8, 6) for chunk in CHUNKS],
    ]
    return pl.pallas_call(
        kernel,
        out_shape=jax.ShapeDtypeStruct((tokens.shape[0], cols), BF16),
        in_specs=[hbm] * 11,
        out_specs=vmem,
        scratch_shapes=scratch,
        compiler_params=pltpu.CompilerParams(
            collective_id=0, has_side_effects=True, vmem_limit_bytes=62 * 2**20
        ),
        name="cross_attention",
    )(
        rows, kv_weight, k_gain.reshape(1, HD), tokens, ln_gain.reshape(8, 8, 128), q_weight,
        q_gain.reshape(1, HD), image_doc, doc_first, doc_count, token_mask.T,
    )


def solution(mesh):
    in_specs = (
        P("cp", None, ("segment", "tp")),
        P(("segment", "tp"), None),
        P(),
        P("cp", ("segment", "tp")),
        P(),
        P(None, ("segment", "tp")),
        P(),
        P(),
        P(),
        P(),
        P("cp", None),
    )
    out_specs = P("cp", ("segment", "tp"))
    return jax.shard_map(
        per_device, mesh=mesh, in_specs=in_specs, out_specs=out_specs, check_vma=False
    )
```
